256 devices in a mesh: row: 8 (over x, z_lo), col: 32 (over z_hi, y, core).
Axes of the slice: x: 4, y: 4, z: 8 (z_hi: 4, z_lo: 2; z = z_hi * 2 + z_lo), core: 2. Of those that a mesh axis runs over, the one named last changes fastest.
Arguments:
- sample_values: float32 [4, 4096], P(None, ('row', 'col')), may hold values from -8 to 8, as said below
- sample_codes: int32 [2, 4096], P(None, ('row', 'col')), may hold values from 0 to 511, as said below
- basis_tables: bfloat16 [2, 512, 12288], P(None, None, 'col'), may hold values from -6 to 6
- model_params: float32 [12288], P('col'), may hold values from -0.0546875 to 0.0546875
- gram_prev: float32 [12288, 12288], P('row', 'col'), may hold values from -6 to 6
- rhs_prev: float32 [12288], P('col'), may hold values from -6 to 6
Outputs:
- gram: float32 [12288, 12288], P('row', 'col')
- rhs: float32 [12288], P('col')
The draws below stay inside these ranges and needn't reach their ends.
Inputs may be any that keep to these rules, and one draw needn't show every extreme that they name: `sample_values`: row 0 and 1 hold direction cosines within -1 to 1, row 2 a log radius ratio within -0.02 to 0.02, row 3 the observed field. `sample_codes`: row 0 holds grid cell ids, row 1 group indices 0 or 1.
All inputs are finite; a program needn't handle non-finite values.
Results may differ from the reference program's by a relative error of at most 0.0029.
Values may be sent and summed in bfloat16 or wider, within the bound.
A program may use at most 128 MiB of HBM per device.

```python
import math
import jax
import jax.numpy as jnp
from jax import lax

P_SIZE = 12288
NCELL = 512
MAXDEG = 64
SAMPLES = 4096


def draw_sample_values(key, part):
    key = jax.random.fold_in(key, 11)
    key_cos, key_ratio, key_obs = jax.random.split(key, 3)
    cosines = jax.random.uniform(key_cos, (2, SAMPLES), jnp.float32, -1.0, 1.0)
    ratio = jax.random.uniform(key_ratio, (1, SAMPLES), jnp.float32, -0.02, 0.02)
    observed = jnp.clip(2.0 * jax.random.normal(key_obs, (1, SAMPLES), jnp.float32), -8.0, 8.0)
    return jnp.concatenate([cosines, ratio, observed], axis=0)


def draw_sample_codes(key, part):
    key = jax.random.fold_in(key, 12)
    key_cell, key_group = jax.random.split(key, 2)
    cell_ids = jax.random.randint(key_cell, (1, SAMPLES), 0, NCELL, jnp.int32)
    group_ids = jax.random.randint(key_group, (1, SAMPLES), 0, 2, jnp.int32)
    return jnp.concatenate([cell_ids, group_ids], axis=0)


def level_of(stream_key, extent, shards, least, largest):
    gain, own = 1.0, jax.random.fold_in(stream_key, 6)
    for axis_at, blocks in shards:
        draws = jnp.exp(jax.random.uniform(jax.random.fold_in(own, axis_at), (blocks,), jnp.float32, least / len(shards), largest / len(shards)))
        gain = gain * jnp.repeat(draws, extent[axis_at] // blocks).reshape([-1 if axis == axis_at else 1 for axis in range(len(extent))])
    return gain


def centred(rng, dims, deviation, most, cuts=(), kind=jnp.bfloat16):
    array = jax.random.normal(rng, dims, jnp.float32) * deviation
    if len(cuts) > 0:
        array = level_of(rng, dims, cuts, -0.22, 0.18) * array
    return jnp.clip(array, min=-most, max=most).astype(kind)


def setup_inputs(seed: int = 0) -> dict:
    seeds = jax.random.split(jax.random.key(seed), 7)
    sample_values = draw_sample_values(jax.random.fold_in(seeds[6], 71), 0)
    sample_codes = draw_sample_codes(jax.random.fold_in(seeds[6], 71), 0)
    basis_tables = centred(seeds[2], (2, NCELL, P_SIZE), 1.0, 6.0, ((2, 32),))
    model_params = centred(seeds[3], (P_SIZE,), P_SIZE ** -0.5, 0.0546875, ((0, 32),), jnp.float32)
    gram_prev = centred(seeds[4], (P_SIZE, P_SIZE), 1.0, 6.0, ((0, 8), (1, 32)), jnp.float32)
    rhs_prev = centred(seeds[5], (P_SIZE,), 1.0, 6.0, ((0, 32),), jnp.float32)
    return {"sample_values": sample_values, "sample_codes": sample_codes, "basis_tables": basis_tables, "model_params": model_params, "gram_prev": gram_prev, "rhs_prev": rhs_prev}


def build_design(tables, cell_ids, geometry, exponent):
    picked = jnp.take(tables, cell_ids, axis=1).astype(jnp.float32)
    mixed_part = geometry[0][:, None] * picked[0] + geometry[1][:, None] * picked[1]
    return mixed_part * jnp.exp(geometry[2][:, None] * exponent[None, :])

def reference(sample_values, sample_codes, basis_tables, model_params, gram_prev, rhs_prev):
    total_rows = sample_values.shape[1]
    block_rows = min(2048, total_rows)
    blocks = total_rows // block_rows
    exponent = (jnp.arange(P_SIZE, dtype=jnp.int32) % MAXDEG + 1).astype(jnp.float32)

    def block_plain(number):
        first = (number * block_rows).astype(jnp.int32)
        cell_ids = lax.dynamic_slice_in_dim(sample_codes[0], first, block_rows)
        geometry = lax.dynamic_slice_in_dim(sample_values, first, block_rows, 1)
        return build_design(basis_tables, cell_ids, geometry, exponent).astype(jnp.bfloat16)

    def predict(number):
        plain = block_plain(number)
        return jnp.dot(plain, model_params, preferred_element_type=jnp.float32, precision=lax.Precision.HIGHEST)
    prediction = lax.map(predict, jnp.arange(blocks, dtype=jnp.int32)).reshape(-1)
    residual = sample_values[3] - prediction
    group_hot = (sample_codes[1][None, :] == jnp.arange(2, dtype=jnp.int32)[:, None]).astype(jnp.float32)
    counts = lax.optimization_barrier(jnp.sum(group_hot, axis=1))
    spread = lax.optimization_barrier(jnp.sum(group_hot * jnp.abs(residual)[None, :], axis=1))
    threshold = 1.345 * spread / jnp.maximum(counts, 1.0)
    limit = lax.optimization_barrier(jnp.sum(group_hot * threshold[:, None], axis=0))
    weights = limit / jnp.maximum(jnp.abs(residual), limit)
    scale = 1.0 / math.sqrt(total_rows)

    def accumulate(number, carry):
        gram_sum, rhs_sum = carry
        first = (number * block_rows).astype(jnp.int32)
        plain = block_plain(number)
        weight_part = lax.dynamic_slice_in_dim(weights, first, block_rows)
        residual_part = lax.dynamic_slice_in_dim(residual, first, block_rows)
        weighted = (weight_part[:, None] * plain.astype(jnp.float32)).astype(jnp.bfloat16)
        gram_sum = gram_sum + lax.dot_general(plain, weighted, (((0,), (0,)), ((), ())), preferred_element_type=jnp.float32)
        rhs_sum = rhs_sum + jnp.dot(residual_part, weighted, preferred_element_type=jnp.float32, precision=lax.Precision.HIGHEST)
        return (gram_sum, rhs_sum)
    start_carry = (jnp.zeros((P_SIZE, P_SIZE), jnp.float32), jnp.zeros((P_SIZE,), jnp.float32))
    gram_sum, rhs_sum = lax.fori_loop(0, blocks, accumulate, start_carry)
    return (gram_prev + scale * gram_sum, rhs_prev + scale * rhs_sum)
```

```python
import functools
import math

import jax
import jax.numpy as jnp
from jax import lax
from jax.experimental import pallas as pl
from jax.experimental.pallas import tpu as pltpu
from jax.sharding import PartitionSpec as P

MAXDEG = 64
MESH = pl.DeviceIdType.MESH
CHUNKS = 4
VMEM_LIMIT = 60 * 1024 * 1024


def exchange_kernel(
    nrow, ncol, width,
    basis_ref, params_ref, samp_ref,
    rows_ref, own_ref, sums_ref, samples_ref,
    part, land1, slot1, tot1, land2, slot2,
    send1, recv1, send2, recv2, send3, recv3,
    sends, recvs, local_sem, stage_recv, fwd_recv, mate_recv, core_recv, fwd_send, stage_send,
):
    nz = ncol // 8
    row, col = lax.axis_index("row"), lax.axis_index("col")
    x, zlo = row // 2, row % 2
    zhi, yk = col // 8, col % 8
    y, core = yk // 2, yk % 2
    ncell = basis_ref.shape[1]
    lanes = sums_ref.shape[2]
    rows_chunk = width // CHUNKS

    def col_of(zh, yy, kk):
        return zh * 8 + yy * 2 + kk

    owner = (y // 2) == zlo
    mate_y = y + 1 - 2 * (y % 2)
    outer_y = (y + 3 + 2 * (y % 2)) % 4
    mate = (row, col_of(zhi, mate_y, core))
    outer = (row, col_of(zhi, outer_y, core))
    sibling = (row, col_of(zhi, y, 1 - core))
    target = (2 * zhi + y // 2, col_of(x, y, core))
    to_self = (zhi == x) & owner
    parity = y % 2
    mine = jnp.where(owner, parity, 1 - parity)
    slot_mine = 2 * mine + core
    slot_mate = 2 * (1 - mine) + core

    barrier = pltpu.get_barrier_semaphore()

    def greet(device):
        pl.semaphore_signal(barrier, inc=1, device_id=device, device_id_type=MESH)

    for d in range(1, 8):
        greet((row, zhi * 8 + (yk + d) % 8))
    for d in range(1, nz):
        greet((row, ((zhi + d) % nz) * 8 + yk))
    for d in range(1, nrow):
        greet(((row + d) % nrow, col))
    for half in range(2):
        @pl.when(owner & ((zhi != x) | (zlo != half)))
        def _():
            greet((2 * zhi + half, col_of(x, y, core)))

    for a in range(2):
        total = None
        for j in range(width // 128):
            block = basis_ref[a, :, 128 * j : 128 * (j + 1)].astype(jnp.float32)
            turned = block.T
            own_ref[128 * j : 128 * (j + 1), a * ncell : (a + 1) * ncell] = turned.astype(jnp.bfloat16)
            term = block * params_ref[:, 128 * j : 128 * (j + 1)]
            total = term if total is None else total + term
        turned = total.T
        both = turned[:MAXDEG] + turned[MAXDEG:]
        per = ncell // lanes
        for i in range(per):
            part[a * per + i] = both[:, i * lanes : (i + 1) * lanes]

    count = 7 + (nz - 1) + (nrow - 1)
    pl.semaphore_wait(barrier, count + 1 - to_self.astype(jnp.int32))

    def remote(src, dst, ssem, rsem, device):
        return pltpu.make_async_remote_copy(
            src_ref=src, dst_ref=dst, send_sem=ssem, recv_sem=rsem, device_id=device, device_id_type=MESH
        )

    first = []
    for d in range(1, 8):
        peer = (row, zhi * 8 + (yk + d) % 8)
        first.append(remote(part.at[row], land1.at[d], send1.at[d], recv1.at[d], peer))
        first.append(remote(samp_ref, slot1.at[yk], sends.at[d], recvs.at[d], peer))
    for copy in first:
        copy.start()

    def table(slot, j):
        return rows_ref.at[slot, pl.ds(rows_chunk * j, rows_chunk)]

    per_half = CHUNKS // 2
    for j in range(CHUNKS):
        half = j // per_half
        source = own_ref.at[pl.ds(rows_chunk * j, rows_chunk)]

        @pl.when((zlo == half) & jnp.logical_not(to_self))
        def _():
            remote(source, table(2 * parity + core, j), stage_send.at[j], stage_recv.at[j], target).start()

        @pl.when((zlo == half) & to_self)
        def _():
            pltpu.make_async_copy(source, table(2 * parity + core, j), stage_recv.at[j]).start()

    slot1[yk] = samp_ref[...]
    for copy in first:
        copy.wait_recv()
    total = part[row]
    for d in range(1, 8):
        total = total + land1[d]
    tot1[...] = total
    for i in range(8):
        slot2[zhi, pl.ds(i, 1)] = slot1[i]

    second = []
    for d in range(1, nz):
        peer = (row, ((zhi + d) % nz) * 8 + yk)
        second.append(remote(tot1, land2.at[d], send2.at[d], recv2.at[d], peer))
        second.append(remote(slot2.at[zhi], slot2.at[zhi], sends.at[7 + d], recvs.at[7 + d], peer))
    for copy in second:
        copy.start()

    def got(j):
        return remote(table(slot_mine, j), table(slot_mine, j), fwd_send.at[0, j], fwd_recv.at[j], mate)

    def pass_mine(j):
        @pl.when(owner)
        def _():
            pltpu.make_async_copy(
                own_ref.at[pl.ds(rows_chunk * j, rows_chunk)], table(slot_mine, j), stage_recv.at[j]
            ).wait()

        @pl.when(jnp.logical_not(owner))
        def _():
            got(j).wait_recv()

        remote(table(slot_mine, j), table(slot_mine, j), fwd_send.at[0, j], mate_recv.at[j], mate).start()

        @pl.when(owner)
        def _():
            remote(table(slot_mine, j), table(slot_mine, j), fwd_send.at[1, j], fwd_recv.at[j], outer).start()

        remote(table(slot_mine, j), table(slot_mine, j), fwd_send.at[2, j], core_recv.at[0, j], sibling).start()

    def pass_mate(j):
        remote(table(slot_mate, j), table(slot_mate, j), fwd_send.at[0, j], mate_recv.at[j], mate).wait_recv()
        remote(table(slot_mate, j), table(slot_mate, j), fwd_send.at[3, j], core_recv.at[1, j], sibling).start()

    pass_mine(0)

    for copy in second:
        copy.wait_recv()
    total = tot1[...]
    for d in range(1, nz):
        total = total + land2[d]
    sums_ref[row] = total
    for i in range(nz):
        samples_ref[row, pl.ds(8 * i, 8)] = slot2[i]

    third = []
    for d in range(1, nrow):
        peer = ((row + d) % nrow, col)
        third.append(remote(sums_ref.at[row], sums_ref.at[row], send3.at[d], recv3.at[d], peer))
        third.append(remote(samples_ref.at[row], samples_ref.at[row], sends.at[10 + d], recvs.at[10 + d], peer))
    for copy in third:
        copy.start()

    for j in range(1, CHUNKS):
        pass_mine(j)
        pass_mate(j - 1)
    pass_mate(CHUNKS - 1)

    for copy in third:
        copy.wait_recv()
    for j in range(CHUNKS):
        remote(table(0, j), table(0, j), fwd_send.at[2, j], core_recv.at[0, j], sibling).wait_recv()
        remote(table(0, j), table(0, j), fwd_send.at[3, j], core_recv.at[1, j], sibling).wait_recv()

    for copy in first + second + third:
        copy.wait_send()
    for j in range(CHUNKS):
        @pl.when((zlo == j // per_half) & jnp.logical_not(to_self))
        def _():
            remote(table(0, j), table(0, j), stage_send.at[j], stage_recv.at[j], target).wait_send()

        for kind in (0, 2, 3):
            remote(table(0, j), table(0, j), fwd_send.at[kind, j], fwd_recv.at[j], mate).wait_send()

        @pl.when(owner)
        def _():
            remote(table(0, j), table(0, j), fwd_send.at[1, j], fwd_recv.at[j], outer).wait_send()


def exchange(nrow, ncol, tables, params, packed):
    ncell, width = tables.shape[1:]
    lanes = 2 * ncell // nrow
    nz = ncol // 8
    dma = pltpu.SemaphoreType.DMA
    vmem = pl.BlockSpec(memory_space=pltpu.VMEM)
    f32, bf16 = jnp.float32, jnp.bfloat16
    return pl.pallas_call(
        functools.partial(exchange_kernel, nrow, ncol, width),
        out_shape=(
            jax.ShapeDtypeStruct((4, width, 2 * ncell), bf16),
            jax.ShapeDtypeStruct((width, 2 * ncell), bf16),
            jax.ShapeDtypeStruct((nrow, MAXDEG, lanes), f32),
            jax.ShapeDtypeStruct((nrow, ncol, 128), f32),
        ),
        in_specs=[vmem] * 3,
        out_specs=(vmem,) * 4,
        scratch_shapes=[
            pltpu.VMEM((nrow, MAXDEG, lanes), f32),
            pltpu.VMEM((8, MAXDEG, lanes), f32),
            pltpu.VMEM((8, 1, 128), f32),
            pltpu.VMEM((MAXDEG, lanes), f32),
            pltpu.VMEM((nz, MAXDEG, lanes), f32),
            pltpu.VMEM((nz, 8, 128), f32),
            dma((8,)), dma((8,)),
            dma((nz,)), dma((nz,)),
            dma((nrow,)), dma((nrow,)),
            dma((20,)), dma((20,)),
            dma, dma((CHUNKS,)), dma((CHUNKS,)), dma((CHUNKS,)), dma((2, CHUNKS)), dma((4, CHUNKS)), dma((CHUNKS,)),
        ],
        compiler_params=pltpu.CompilerParams(
            collective_id=0, has_side_effects=True, vmem_limit_bytes=VMEM_LIMIT
        ),
    )(tables, params, packed)


TILE = 256


def normal_kernel(
    scale,
    rows_ref, own_ref, sums_ref, samples_ref, gram_prev_ref, rhs_prev_ref,
    gram_ref, rhs_ref,
    turned, pieces, grown, hots, pred, design, weighted, plain, extra,
):
    f32, bf16 = jnp.float32, jnp.bfloat16
    ncell = rows_ref.shape[2] // 2
    width = own_ref.shape[0]
    ndev = samples_ref.shape[0]
    nrow, _, lanes = sums_ref.shape
    tiles = pred.shape[0]
    per = nrow // 2
    turned[...] = samples_ref[...].T
    for a in range(2):
        for i in range(per):
            value = sums_ref[a * per + i]
            for n in range(3):
                piece = value.astype(bf16)
                pieces[a, n * MAXDEG : (n + 1) * MAXDEG, i * lanes : (i + 1) * lanes] = piece
                value = value - piece.astype(f32)

    exponent = (lax.broadcasted_iota(jnp.int32, (MAXDEG, TILE), 0) + 1).astype(f32)
    cells = lax.broadcasted_iota(jnp.int32, (ncell, TILE), 0)

    def field(number, k):
        return turned[pl.ds(number * tiles + k, 1), :]

    def prepare(k, carry):
        grow = jnp.exp(field(2, k) * exponent)
        grown[0, k] = grow * field(0, k)
        grown[1, k] = grow * field(1, k)
        hot = (cells == field(4, k).astype(jnp.int32)).astype(f32).astype(bf16)
        hots[k] = hot
        value = None
        for a in range(2):
            picked = jnp.dot(pieces[a], hot, preferred_element_type=f32)
            term = grown[a, k] * (
                picked[:MAXDEG] + picked[MAXDEG : 2 * MAXDEG] + picked[2 * MAXDEG :]
            )
            value = term if value is None else value + term
        pred[pl.ds(k, 1), :] = jnp.sum(value, axis=0, keepdims=True)
        return carry

    lax.fori_loop(0, tiles, prepare, 0)

    residual = turned[3 * tiles : 4 * tiles, :] - pred[...]
    group = turned[5 * tiles : 6 * tiles, :]
    size = jnp.abs(residual)
    limit = jnp.zeros_like(size)
    for number in range(2):
        hot = (group == float(number)).astype(f32)
        count = jnp.sum(jnp.sum(hot, axis=0, keepdims=True), axis=1, keepdims=True)
        spread = jnp.sum(jnp.sum(hot * size, axis=0, keepdims=True), axis=1, keepdims=True)
        limit = limit + hot * (1.345 * spread / jnp.maximum(count, 1.0))
    weights = limit / jnp.maximum(size, limit)
    turned[3 * tiles : 4 * tiles, :] = residual
    turned[5 * tiles : 6 * tiles, :] = weights

    def build(k, carry):
        hot = hots[k]
        first, second = grown[0, k], grown[1, k]
        at = pl.ds(pl.multiple_of(k * TILE, TILE), TILE)

        def designed(table):
            east = jnp.dot(table[:, :ncell], hot, preferred_element_type=f32)
            north = jnp.dot(table[:, ncell:], hot, preferred_element_type=f32)
            return [
                (
                    east[MAXDEG * i : MAXDEG * (i + 1)] * first
                    + north[MAXDEG * i : MAXDEG * (i + 1)] * second
                ).astype(bf16)
                for i in range(table.shape[0] // MAXDEG)
            ]

        weight = field(5, k)
        for i, block in enumerate(designed(own_ref[...])):
            weighted[MAXDEG * i : MAXDEG * (i + 1), at] = (block.astype(f32) * weight).astype(bf16)
        for t in range(4):
            for i, block in enumerate(designed(rows_ref[t])):
                design[pl.ds(t * width + MAXDEG * i, MAXDEG), at] = block
        value = field(3, k)
        for n in range(3):
            piece = value.astype(bf16).astype(f32)
            extra[pl.ds(n, 1), at] = piece
            value = value - piece
        return carry

    extra[...] = jnp.zeros_like(extra)
    lax.fori_loop(0, tiles, build, 0)

    nt = (((1,), (1,)), ((), ()))

    def gram_step(i, carry):
        at = pl.ds(pl.multiple_of(i * width, width), width)
        product = lax.dot_general(design[at, :], weighted[...], nt, preferred_element_type=f32)
        gram_ref[at, :] = gram_prev_ref[at, :] + scale * product
        return carry

    lax.fori_loop(0, 4, gram_step, 0)
    side = lax.dot_general(extra[...].astype(bf16), weighted[...], nt, preferred_element_type=f32)
    rhs_ref[...] = rhs_prev_ref[...] + scale * jnp.sum(side[:8], axis=0, keepdims=True)


def normal(tables_rows, table_own, sums, samples, gram_prev, rhs_prev):
    f32, bf16 = jnp.float32, jnp.bfloat16
    ndev = samples.shape[0]
    tiles = samples.shape[0] * 16 // TILE
    total = tiles * TILE
    ncell = table_own.shape[1] // 2
    width = table_own.shape[0]
    vmem = pl.BlockSpec(memory_space=pltpu.VMEM)
    return pl.pallas_call(
        functools.partial(normal_kernel, 1.0 / math.sqrt(total)),
        out_shape=(
            jax.ShapeDtypeStruct(gram_prev.shape, f32),
            jax.ShapeDtypeStruct(rhs_prev.shape, f32),
        ),
        in_specs=[vmem] * 6,
        out_specs=(vmem, vmem),
        scratch_shapes=[
            pltpu.VMEM((128, ndev), f32),
            pltpu.VMEM((2, 3 * MAXDEG, ncell), bf16),
            pltpu.VMEM((2, tiles, MAXDEG, TILE), f32),
            pltpu.VMEM((tiles, ncell, TILE), bf16),
            pltpu.VMEM((tiles, TILE), f32),
            pltpu.VMEM((4 * width, total), bf16),
            pltpu.VMEM((width, total), bf16),
            pltpu.VMEM((8, 128), f32),
            pltpu.VMEM((16, total), f32),
        ],
        compiler_params=pltpu.CompilerParams(vmem_limit_bytes=VMEM_LIMIT),
    )(tables_rows, table_own, sums, samples, gram_prev, rhs_prev)


def local(nrow, ncol, sample_values, sample_codes, basis_tables, model_params, gram_prev, rhs_prev):
    width = basis_tables.shape[2]
    packed = jnp.concatenate(
        [
            sample_values.reshape(1, -1),
            sample_codes.astype(jnp.float32).reshape(1, -1),
            jnp.zeros((1, 32), jnp.float32),
        ],
        axis=1,
    )
    rows, own, sums, samples = exchange(nrow, ncol, basis_tables, model_params.reshape(1, width), packed)
    gram, rhs = normal(rows, own, sums, samples.reshape(nrow * ncol, 128), gram_prev, rhs_prev.reshape(1, width))
    return (gram, rhs.reshape(width))


def solution(mesh):
    placed = (
        P(None, ("row", "col")),
        P(None, ("row", "col")),
        P(None, None, "col"),
        P("col"),
        P("row", "col"),
        P("col"),
    )
    return jax.shard_map(
        functools.partial(local, mesh.shape["row"], mesh.shape["col"]),
        mesh=mesh,
        in_specs=placed,
        out_specs=(P("row", "col"), P("col")),
        check_vma=False,
    )
```

```python
import functools
import math

import jax
import jax.numpy as jnp
from jax import lax
from jax.experimental import pallas as pl
from jax.experimental.pallas import tpu as pltpu
from jax.sharding import PartitionSpec as P

MAXDEG = 64
MESH = pl.DeviceIdType.MESH
VMEM_LIMIT = 60 * 1024 * 1024
NT = (((1,), (1,)), ((), ()))
SIDE = 16


def kernel(
    nrow, ncol,
    basis_ref, params_ref, values_ref, codes_ref, prev_ref, rhs_prev_ref,
    gram_ref, rhs_ref,
    own, tab, zbuf, part, land1, tot1, land2, sums, slots, samples,
    turned, pieces, grown, hots, pred, design, weighted, gram, away, back,
    s1_send, s1_recv, s2_send, s2_recv,
    g1_send, g1_recv, g2_send, g2_recv, g3_send, g3_recv,
    z_send, z_recv, x_send, x_recv, y_send, outer_recv, mate_recv,
    w_send, w_recv, p_send, p_recv, prev_sem, out_sem,
):
    f32, bf16 = jnp.float32, jnp.bfloat16
    nz = ncol // 8
    row, col = lax.axis_index("row"), lax.axis_index("col")
    x, zlo = row // 2, row % 2
    zhi, yk = col // 8, col % 8
    y, core = yk // 2, yk % 2
    ncell, width = basis_ref.shape[1:]
    lanes = sums.shape[2]
    piece = width // nrow
    tiles = values_ref.shape[1]
    tile = nrow * ncol
    total = tiles * tile
    scale = 1.0 / math.sqrt(total)

    def remote(src, dst, ssem, rsem, device):
        return pltpu.make_async_remote_copy(
            src_ref=src, dst_ref=dst, send_sem=ssem, recv_sem=rsem, device_id=device, device_id_type=MESH
        )

    owner = (y // 2) == zlo
    mate = (row, zhi * 8 + 2 * (y + 1 - 2 * (y % 2)) + core)
    outer = (row, zhi * 8 + 2 * ((y + 3 + 2 * (y % 2)) % 4) + core)
    sibling = (row, zhi * 8 + 2 * y + 1 - core)
    col_peers = [(row, (col + d) % ncol) for d in range(ncol)]
    row_peers = [((row + d) % nrow, col) for d in range(nrow)]
    near = [(row, zhi * 8 + (yk + d) % 8) for d in range(8)]
    far = [(row, ((zhi + d) % nz) * 8 + yk) for d in range(nz)]
    other = row + 1 - 2 * zlo
    hand = [(other, far[d][1]) if 2 * d == nz else far[d] for d in range(nz)]
    handed = [other if 2 * d == nz else row for d in range(nz)]
    parity = y % 2
    mine = jnp.where(owner, parity, 1 - parity)

    barrier = pltpu.get_barrier_semaphore()
    greeted = col_peers[1:] + row_peers[1:] + [hand[d] for d in range(1, nz) if 2 * d == nz]
    for peer in greeted:
        pl.semaphore_signal(barrier, inc=1, device_id=peer, device_id_type=MESH)

    prev_copy = pltpu.make_async_copy(prev_ref, gram, prev_sem)
    prev_copy.start()

    slots[row] = jnp.concatenate(
        [values_ref[i : i + 1, :] for i in range(4)]
        + [codes_ref[i : i + 1, :].astype(f32) for i in range(2)]
        + [jnp.zeros((1, 128 - 6 * tiles), f32)],
        axis=1,
    )
    params = params_ref[...].reshape(1, width)
    for a in range(2):
        turns = []
        amount = None
        for j in range(width // 128):
            block = basis_ref[a, :, 128 * j : 128 * (j + 1)].astype(f32)
            turns.append(block.T)
            term = block * params[:, 128 * j : 128 * (j + 1)]
            amount = term if amount is None else amount + term
        whole = jnp.concatenate(turns, axis=0).astype(bf16)
        for p in range(nrow):
            own[p, a * piece : (a + 1) * piece, :] = whole[piece * p : piece * (p + 1)]
        amount = amount.T
        amount = amount[:MAXDEG] + amount[MAXDEG:]
        per = ncell // lanes
        for i in range(per):
            part[a * per + i] = amount[:, i * lanes : (i + 1) * lanes]

    pl.semaphore_wait(barrier, len(greeted))

    s1 = [remote(slots.at[row], slots.at[row], s1_send.at[d], s1_recv.at[d], row_peers[d]) for d in range(1, nrow)]
    for copy in s1:
        copy.start()

    zs = [remote(own.at[row], zbuf.at[nz - d], z_send.at[d], z_recv.at[nz - d], hand[d]) for d in range(1, nz)]
    for copy in zs:
        copy.start()

    def pass_x(d):
        to = 2 * ((zhi + d) % nz) + y // 2
        source = own.at[row] if d == 0 else zbuf.at[d]
        i = (handed[d] - to + nrow) % nrow
        place = tab.at[i, parity]

        @pl.when(to != row)
        def _():
            remote(source, place, x_send.at[d], x_recv.at[i], (to, col)).start()

        @pl.when(to == row)
        def _():
            pltpu.make_async_copy(source, place, x_recv.at[i]).start()

    pass_x(0)
    g1 = [remote(part.at[row], land1.at[d], g1_send.at[d], g1_recv.at[d], near[d]) for d in range(1, 8)]
    for copy in g1:
        copy.start()

    for copy in s1:
        copy.wait_recv()
    for i in range(nrow):
        samples[col, pl.ds(i, 1)] = slots[i]
    s2 = [
        remote(samples.at[col], samples.at[col], s2_send.at[d], s2_recv.at[d], col_peers[d]) for d in range(1, ncol)
    ]
    for copy in s2:
        copy.start()

    for d in range(1, nz):
        remote(zbuf.at[d], zbuf.at[d], z_send.at[d], z_recv.at[d], hand[d]).wait_recv()
        pass_x(d)

    def pass_y(i):
        here = tab.at[i, mine]

        @pl.when(owner)
        def _():
            pltpu.make_async_copy(here, here, x_recv.at[i]).wait()
            remote(here, here, y_send.at[1, i], outer_recv.at[i], outer).start()

        @pl.when(jnp.logical_not(owner))
        def _():
            remote(here, here, y_send.at[1, i], outer_recv.at[i], outer).wait_recv()

        remote(here, here, y_send.at[0, i], mate_recv.at[i], mate).start()

    def wait_mate(i):
        here = tab.at[i, 1 - mine]
        remote(here, here, y_send.at[0, i], mate_recv.at[i], mate).wait_recv()

    def field(number, k):
        return turned[pl.ds(number * tiles + k, 1), :]

    def span(k):
        return pl.ds(pl.multiple_of(k * tile, tile), tile)

    exponent = (lax.broadcasted_iota(jnp.int32, (MAXDEG, tile), 0) + 1).astype(f32)
    cells = lax.broadcasted_iota(jnp.int32, (ncell, tile), 0)
    reach = grown.shape[2]

    def prepare(k, carry):
        grow = jnp.exp(field(2, k) * exponent)
        for a in range(2):
            value = grow * field(a, k)
            for first in range(0, reach, MAXDEG):
                size = min(MAXDEG, reach - first)
                grown[a, k, first : first + size] = value[:size]
        hots[k] = (cells == field(4, k).astype(jnp.int32)).astype(f32).astype(bf16)
        return carry

    def mixed(picked, k, p):
        at = pl.ds(pl.multiple_of((p * piece) % MAXDEG, 16), piece)
        return (picked[:piece] * grown[0, k, at] + picked[piece:] * grown[1, k, at]).astype(bf16)

    def build_own(k, carry):
        picked = jnp.dot(own[...].reshape(2 * width, ncell), hots[k], preferred_element_type=f32)
        for p in range(nrow):
            weighted[0, p * piece : (p + 1) * piece, span(k)] = mixed(
                picked[2 * piece * p : 2 * piece * (p + 1)], k, p
            )
        return carry

    def predict(k, carry):
        value = None
        for a in range(2):
            picked = jnp.dot(pieces[a], hots[k], preferred_element_type=f32)
            term = grown[a, k, :MAXDEG] * (
                picked[:MAXDEG] + picked[MAXDEG : 2 * MAXDEG] + picked[2 * MAXDEG :]
            )
            value = term if value is None else value + term
        pred[pl.ds(k, 1), :] = jnp.sum(value, axis=0, keepdims=True)
        return carry

    def weigh(k, carry):
        weighted[0, :, span(k)] = (weighted[0, :, span(k)].astype(f32) * field(5, k)).astype(bf16)
        rest = field(3, k)
        split = []
        for n in range(3):
            split.append(rest.astype(bf16).astype(f32))
            rest = rest - split[-1]
        split.append(jnp.zeros((SIDE - 3, tile), f32))
        design[width : width + SIDE, span(k)] = jnp.concatenate(split, axis=0).astype(bf16)
        return carry

    step = max(1, nrow // 4)

    def build_rows(unit):
        def body(k, carry):
            lhs = tab[step * unit : step * (unit + 1)].reshape(step * 4 * piece, ncell)
            picked = jnp.dot(lhs, hots[k], preferred_element_type=f32)
            for n in range(step):
                i = step * unit + n
                for par in range(2):
                    first = (2 * n + par) * 2 * piece
                    at = (2 * i + par) * piece + (SIDE if 2 * i >= nrow else 0)
                    design[at : at + piece, span(k)] = mixed(
                        picked[first : first + 2 * piece], k, (row + i) % nrow
                    )
            return carry

        lax.fori_loop(0, tiles, body, 0, unroll=2)

    def place(i, par, which):
        return pl.ds(pl.multiple_of((2 * par + which) * width + ((row + i) % nrow) * piece, 16), piece)

    def out_copy(i, par, which):
        at = place(i, par, which)
        return pltpu.make_async_copy(gram.at[at], gram_ref.at[at], out_sem.at[i, par, which])

    half = nrow // 2

    def form(h):
        rows = width + (SIDE if h == 0 else 0)
        first = 0 if h == 0 else width + SIDE
        both = weighted[...].reshape(2 * width, total)
        product = lax.dot_general(design[first : first + rows], both, NT, preferred_element_type=f32)
        away[h] = product[:width, width:]
        remote(away.at[h], back.at[h], p_send.at[h], p_recv.at[h], sibling).start()
        for n in range(half):
            for par in range(2):
                at = place(half * h + n, par, core)
                begin = (2 * n + par) * piece
                gram[at, :] = gram[at, :] + scale * product[begin : begin + piece, :width]
                out_copy(half * h + n, par, core).start()
        if h == 0:
            rhs_ref[...] = rhs_prev_ref[...] + scale * jnp.sum(product[width : width + 8, :width], axis=0)

    def finish(h):
        remote(away.at[h], back.at[h], p_send.at[h], p_recv.at[h], sibling).wait_recv()
        for n in range(half):
            for par in range(2):
                at = place(half * h + n, par, 1 - core)
                begin = (2 * n + par) * piece
                gram[at, :] = gram[at, :] + scale * back[h, begin : begin + piece, :]
                out_copy(half * h + n, par, 1 - core).start()

    def some(body, number, parts):
        lax.fori_loop(number * tiles // parts, (number + 1) * tiles // parts, body, 0, unroll=2)

    pass_y(0)
    for copy in g1:
        copy.wait_recv()
    amount = part[row]
    for d in range(1, 8):
        amount = amount + land1[d]
    tot1[...] = amount
    g2 = [remote(tot1, land2.at[d], g2_send.at[d], g2_recv.at[d], far[d]) for d in range(1, nz)]
    for copy in g2:
        copy.start()

    for copy in s2:
        copy.wait_recv()
    turned[...] = samples[...].reshape(tile, 128).T
    for n in range(4):
        some(prepare, n, 4)
        if n + 1 < nrow:
            pass_y(n + 1)
        if n == 1:
            for copy in g2:
                copy.wait_recv()
            amount = tot1[...]
            for d in range(1, nz):
                amount = amount + land2[d]
            sums[row] = amount
            g3 = [
                remote(sums.at[row], sums.at[row], g3_send.at[d], g3_recv.at[d], row_peers[d])
                for d in range(1, nrow)
            ]
            for copy in g3:
                copy.start()
    for n in range(4):
        some(build_own, n, 4)
        if n + 5 < nrow:
            pass_y(n + 5)

    for copy in g3:
        copy.wait_recv()
    per = nrow // 2
    for a in range(2):
        for i in range(per):
            value = sums[a * per + i]
            for n in range(3):
                part_value = value.astype(bf16)
                pieces[a, n * MAXDEG : (n + 1) * MAXDEG, i * lanes : (i + 1) * lanes] = part_value
                value = value - part_value.astype(f32)
    some(predict, 0, 1)

    residual = turned[3 * tiles : 4 * tiles, :] - pred[...]
    group = turned[5 * tiles : 6 * tiles, :]
    size = jnp.abs(residual)
    limit = jnp.zeros_like(size)
    for number in range(2):
        hot = (group == float(number)).astype(f32)
        count = jnp.sum(jnp.sum(hot, axis=0, keepdims=True), axis=1, keepdims=True)
        spread = jnp.sum(jnp.sum(hot * size, axis=0, keepdims=True), axis=1, keepdims=True)
        limit = limit + hot * (1.345 * spread / jnp.maximum(count, 1.0))
    turned[3 * tiles : 4 * tiles, :] = residual
    turned[5 * tiles : 6 * tiles, :] = limit / jnp.maximum(size, limit)
    some(weigh, 0, 1)
    w_copy = remote(weighted.at[0], weighted.at[1], w_send, w_recv, sibling)
    w_copy.start()

    units = nrow // step
    for unit in range(units):
        for i in range(step * unit, step * (unit + 1)):
            wait_mate(i)
        build_rows(unit)
        if unit + 1 == units // 2:
            w_copy.wait_recv()
            prev_copy.wait()
            form(0)
        if unit + 2 == units:
            finish(0)
    form(1)
    finish(1)

    for copy in s1 + s2 + g1 + g2 + g3 + zs + [w_copy]:
        copy.wait_send()
    for d in range(nz):
        to = 2 * ((zhi + d) % nz) + y // 2

        @pl.when(to != row)
        def _():
            remote(own.at[row], own.at[row], x_send.at[d], x_recv.at[0], (to, col)).wait_send()

    for i in range(nrow):
        here = tab.at[i, 0]
        remote(here, here, y_send.at[0, i], mate_recv.at[i], mate).wait_send()

        @pl.when(owner)
        def _():
            remote(here, here, y_send.at[1, i], outer_recv.at[i], outer).wait_send()

    for h in range(2):
        remote(away.at[h], back.at[h], p_send.at[h], p_recv.at[h], sibling).wait_send()
    for i in range(nrow):
        for par in range(2):
            for which in (core, 1 - core):
                out_copy(i, par, which).wait()


def local(nrow, ncol, sample_values, sample_codes, basis_tables, model_params, gram_prev, rhs_prev):
    ncell, width = basis_tables.shape[1:]
    lanes = 2 * ncell // nrow
    nz = ncol // 8
    tiles = sample_values.shape[1]
    tile = nrow * ncol
    total = tile * tiles
    piece = width // nrow
    dma = pltpu.SemaphoreType.DMA
    vmem = pl.BlockSpec(memory_space=pltpu.VMEM)
    anywhere = pl.BlockSpec(memory_space=pl.ANY)
    f32, bf16 = jnp.float32, jnp.bfloat16
    return pl.pallas_call(
        functools.partial(kernel, nrow, ncol),
        out_shape=(
            jax.ShapeDtypeStruct(gram_prev.shape, f32),
            jax.ShapeDtypeStruct(rhs_prev.shape, f32),
        ),
        in_specs=[vmem, vmem, vmem, vmem, anywhere, vmem],
        out_specs=(anywhere, vmem),
        scratch_shapes=[
            pltpu.VMEM((nrow, 2 * piece, ncell), bf16),
            pltpu.VMEM((nrow, 2, 2 * piece, ncell), bf16),
            pltpu.VMEM((nz, 2 * piece, ncell), bf16),
            pltpu.VMEM((nrow, MAXDEG, lanes), f32),
            pltpu.VMEM((8, MAXDEG, lanes), f32),
            pltpu.VMEM((MAXDEG, lanes), f32),
            pltpu.VMEM((nz, MAXDEG, lanes), f32),
            pltpu.VMEM((nrow, MAXDEG, lanes), f32),
            pltpu.VMEM((nrow, 1, 128), f32),
            pltpu.VMEM((ncol, nrow, 128), f32),
            pltpu.VMEM((128, tile), f32),
            pltpu.VMEM((2, 3 * MAXDEG, ncell), bf16),
            pltpu.VMEM((2, tiles, MAXDEG + piece, tile), f32),
            pltpu.VMEM((tiles, ncell, tile), bf16),
            pltpu.VMEM((tiles, tile), f32),
            pltpu.VMEM((2 * width + SIDE, total), bf16),
            pltpu.VMEM((2, width, total), bf16),
            pltpu.VMEM(gram_prev.shape, f32),
            pltpu.VMEM((2, width, width), f32),
            pltpu.VMEM((2, width, width), f32),
            dma((nrow,)), dma((nrow,)), dma((ncol,)), dma((ncol,)),
            dma((8,)), dma((8,)), dma((nz,)), dma((nz,)), dma((nrow,)), dma((nrow,)),
            dma((nz,)), dma((nz,)), dma((nz,)), dma((nrow,)), dma((2, nrow)), dma((nrow,)), dma((nrow,)),
            dma, dma, dma((2,)), dma((2,)), dma, dma((nrow, 2, 2)),
        ],
        compiler_params=pltpu.CompilerParams(
            collective_id=0, has_side_effects=True, vmem_limit_bytes=VMEM_LIMIT
        ),
    )(basis_tables, model_params, sample_values, sample_codes, gram_prev, rhs_prev)


def solution(mesh):
    placed = (
        P(None, ("row", "col")),
        P(None, ("row", "col")),
        P(None, None, "col"),
        P("col"),
        P("row", "col"),
        P("col"),
    )
    return jax.shard_map(
        functools.partial(local, mesh.shape["row"], mesh.shape["col"]),
        mesh=mesh,
        in_specs=placed,
        out_specs=(P("row", "col"), P("col")),
        check_vma=False,
    )
```

```python
import functools
import math

import jax
import jax.numpy as jnp
from jax import lax
from jax.experimental import pallas as pl
from jax.experimental.pallas import tpu as pltpu
from jax.sharding import PartitionSpec as P

MAXDEG = 64
MESH = pl.DeviceIdType.MESH
VMEM_LIMIT = 52 * 1024 * 1024
NT = (((1,), (1,)), ((), ()))
SIDE = 16
PIECES = 8


def kernel(
    nrow, ncol,
    basis_ref, params_ref, values_ref, codes_ref, prev_ref, rhs_prev_ref,
    gram_ref, rhs_ref,
    own, tab, zbuf, part, land1, tot1, land2, sums, slots, samples,
    turned, pieces, grown, hots, pred, design, weighted, away, back,
    s1_send, s1_recv, s2_send, s2_recv,
    g1_send, g1_recv, g2_send, g2_recv, g3_send, g3_recv,
    z_send, z_recv, x_send, x_recv, y_send, y_recv,
    w_send, w_recv, p_send, p_recv, prev_sem,
):
    f32, bf16 = jnp.float32, jnp.bfloat16
    nz = ncol // 8
    row, col = lax.axis_index("row"), lax.axis_index("col")
    x, zlo = row // 2, row % 2
    zhi, yk = col // 8, col % 8
    y, core = yk // 2, yk % 2
    ncell, width = basis_ref.shape[1:]
    lanes = sums.shape[2]
    piece = width // PIECES
    share = PIECES // nrow
    tiles = values_ref.shape[1]
    tile = nrow * ncol
    total = tiles * tile
    scale = 1.0 / math.sqrt(total)

    def remote(src, dst, ssem, rsem, device):
        return pltpu.make_async_remote_copy(
            src_ref=src, dst_ref=dst, send_sem=ssem, recv_sem=rsem, device_id=device, device_id_type=MESH
        )

    left = (row, zhi * 8 + 2 * ((y + 3) % 4) + core)
    right = (row, zhi * 8 + 2 * ((y + 1) % 4) + core)
    sibling = (row, zhi * 8 + 2 * y + 1 - core)
    col_peers = [(row, (col + d) % ncol) for d in range(ncol)]
    row_peers = [((row + d) % nrow, col) for d in range(nrow)]
    near = [(row, zhi * 8 + (yk + d) % 8) for d in range(8)]
    far = [(row, ((zhi + d) % nz) * 8 + yk) for d in range(nz)]
    other = row + 1 - 2 * zlo
    hand = [(other, far[d][1]) if 2 * d == nz else far[d] for d in range(nz)]
    handed = [other if 2 * d == nz else row for d in range(nz)]
    parity = y % 2
    blocks = [(par, e) for par in range(2) for e in range(2)]
    offsets = (0, 3, 1, 2)

    barrier = pltpu.get_barrier_semaphore()
    greeted = col_peers[1:] + row_peers[1:] + [hand[d] for d in range(1, nz) if 2 * d == nz]
    for peer in greeted:
        pl.semaphore_signal(barrier, inc=1, device_id=peer, device_id_type=MESH)

    selves = 0
    for par, e in blocks:
        giver = (2 * y + e) // share
        if nz > 1:
            giver = jnp.where(2 * ((x - zhi + nz) % nz) == nz, giver + 1 - 2 * (giver % 2), giver)
        place = zhi * 8 + 2 * (2 * zlo + par) + core
        to_self = (giver == row) & (place == col)
        selves = selves + to_self.astype(jnp.int32)

        @pl.when(jnp.logical_not(to_self))
        def _():
            pl.semaphore_signal(barrier, inc=1, device_id=(giver, place), device_id_type=MESH)

    prev_copy = pltpu.make_async_copy(prev_ref, gram_ref, prev_sem)
    prev_copy.start()

    slots[row] = jnp.concatenate(
        [values_ref[i : i + 1, :] for i in range(4)]
        + [codes_ref[i : i + 1, :].astype(f32) for i in range(2)]
        + [jnp.zeros((1, 128 - 6 * tiles), f32)],
        axis=1,
    )
    for a in range(2):
        whole = jnp.concatenate(
            [basis_ref[a, :, 128 * j : 128 * (j + 1)].astype(f32).T for j in range(width // 128)], axis=0
        ).astype(bf16)
        for p in range(PIECES):
            own[p, a] = whole[piece * p : piece * (p + 1)]

    pl.semaphore_wait(barrier, len(greeted) + len(blocks) - selves)

    s1 = [remote(slots.at[row], slots.at[row], s1_send.at[d], s1_recv.at[d], row_peers[d]) for d in range(1, nrow)]
    for copy in s1:
        copy.start()

    def pass_z(d, u):
        return [
            remote(own.at[row * share + m, u], zbuf.at[nz - d, m, u], z_send.at[d, m, u], z_recv.at[nz - d, m, u], hand[d])
            for m in range(share)
        ]

    def pass_x(d, u):
        to = 2 * ((zhi + d) % nz) + y // 2
        for m in range(share):
            p = handed[d] * share + m
            target = zhi * 8 + 2 * (p // 2) + core
            source = own.at[p, u] if d == 0 else zbuf.at[d, m, u]
            place = tab.at[0, parity, p % 2, u]
            arrived = x_recv.at[parity, p % 2, u]
            to_self = (to == row) & (target == col)

            @pl.when(jnp.logical_not(to_self))
            def _():
                remote(source, place, x_send.at[d, m, u], arrived, (to, target)).start()

            @pl.when(to_self)
            def _():
                pltpu.make_async_copy(source, place, arrived).start()

    zs = []
    for u in range(2):
        for d in range(1, nz):
            zs += pass_z(d, u)
    for copy in zs:
        copy.start()
    for u in range(2):
        pass_x(0, u)

    params = params_ref[...].reshape(1, width)
    per = ncell // lanes
    for a in range(2):
        amount = None
        for j in range(width // 128):
            term = basis_ref[a, :, 128 * j : 128 * (j + 1)].astype(f32) * params[:, 128 * j : 128 * (j + 1)]
            amount = term if amount is None else amount + term
        amount = amount.T
        amount = amount[:MAXDEG] + amount[MAXDEG:]
        for i in range(per):
            part[a * per + i] = amount[:, i * lanes : (i + 1) * lanes]
    g1 = [remote(part.at[row], land1.at[d], g1_send.at[d], g1_recv.at[d], near[d]) for d in range(1, 8)]
    for copy in g1:
        copy.start()

    for copy in s1:
        copy.wait_recv()
    for i in range(nrow):
        samples[col, pl.ds(i, 1)] = slots[i]
    s2 = [
        remote(samples.at[col], samples.at[col], s2_send.at[d], s2_recv.at[d], col_peers[d]) for d in range(1, ncol)
    ]
    for copy in s2:
        copy.start()

    for u in range(2):
        for d in range(1, nz):
            for m in range(share):
                here = zbuf.at[d, m, u]
                remote(here, here, z_send.at[d, m, u], z_recv.at[d, m, u], hand[d]).wait_recv()
            pass_x(d, u)

    def pass_y(u):
        for par, e in blocks:
            here = tab.at[0, par, e, u]
            pltpu.make_async_copy(here, here, x_recv.at[par, e, u]).wait()
            remote(here, tab.at[1, par, e, u], y_send.at[0, par, e, u], y_recv.at[0, par, e, u], right).start()
            remote(here, tab.at[2, par, e, u], y_send.at[1, par, e, u], y_recv.at[1, par, e, u], left).start()

    def arrive(g, par, e, u):
        here = tab.at[g, par, e, u]
        remote(here, here, y_send.at[0, par, e, u], y_recv.at[g - 1, par, e, u], right).wait_recv()

    def pass_on(u):
        for par in range(2):
            for g, to in ((1, right), (2, left)):
                e = g - 1
                arrive(g, par, e, u)
                remote(
                    tab.at[g, par, e, u], tab.at[3, par, e, u], y_send.at[2, par, e, u], y_recv.at[2, par, e, u], to
                ).start()

    def field(number, k):
        return turned[pl.ds(number * tiles + k, 1), :]

    def span(k):
        return pl.ds(pl.multiple_of(k * tile, tile), tile)

    exponent = (lax.broadcasted_iota(jnp.int32, (MAXDEG, tile), 0) + 1).astype(f32)
    cells = lax.broadcasted_iota(jnp.int32, (ncell, tile), 0).astype(jnp.int16)
    reach = grown.shape[2]

    def build_own(k, carry):
        hot = jnp.where(cells == field(4, k).astype(jnp.int32).astype(jnp.int16), jnp.bfloat16(1), jnp.bfloat16(0))
        hots[k] = hot
        grow = jnp.exp(field(2, k) * exponent)
        grows = []
        for a in range(2):
            value = grow * field(a, k)
            value = jnp.concatenate([value, value], axis=0)
            grown[a, k] = value[:reach]
            grows.append(value)
        picked = jnp.dot(own[...].reshape(2 * width, ncell), hot, preferred_element_type=f32)
        for p in range(PIECES):
            first = 2 * piece * p
            at = (p * piece) % MAXDEG
            weighted[0, p * piece : (p + 1) * piece, span(k)] = (
                picked[first : first + piece] * grows[0][at : at + piece]
                + picked[first + piece : first + 2 * piece] * grows[1][at : at + piece]
            ).astype(bf16)
        return carry

    def mixed(picked, k, p):
        at = pl.ds(pl.multiple_of((p * piece) % MAXDEG, 16), piece)
        return (picked[:piece] * grown[0, k, at] + picked[piece:] * grown[1, k, at]).astype(bf16)

    def predict(picked, k):
        value = None
        for a in range(2):
            three = picked[3 * MAXDEG * a : 3 * MAXDEG * (a + 1)]
            term = grown[a, k, :MAXDEG] * (three[:MAXDEG] + three[MAXDEG : 2 * MAXDEG] + three[2 * MAXDEG :])
            value = term if value is None else value + term
        pred[pl.ds(k, 1), :] = jnp.sum(value, axis=0, keepdims=True)

    def weigh(k, carry):
        weighted[0, :, span(k)] = (weighted[0, :, span(k)].astype(f32) * field(5, k)).astype(bf16)
        rest = field(3, k)
        split = []
        for n in range(3):
            split.append(rest.astype(bf16).astype(f32))
            rest = rest - split[-1]
        split.append(jnp.zeros((SIDE - 3, tile), f32))
        design[width : width + SIDE, span(k)] = jnp.concatenate(split, axis=0).astype(bf16)
        return carry

    def origin(g, e):
        return 2 * ((y + offsets[g]) % 4) + e

    def build_rows(g):
        def body(k, carry):
            lhs = tab[g].reshape(8 * piece, ncell)
            if g == 0:
                lhs = jnp.concatenate([lhs, pieces[...].reshape(6 * MAXDEG, ncell)], axis=0)
            picked = jnp.dot(lhs, hots[k], preferred_element_type=f32)
            if g == 0:
                predict(picked[8 * piece :], k)
            for n, (par, e) in enumerate(blocks):
                at = (4 * g + n) * piece + (SIDE if g >= 2 else 0)
                design[at : at + piece, span(k)] = mixed(picked[2 * piece * n : 2 * piece * (n + 1)], k, origin(g, e))
            return carry

        lax.fori_loop(0, tiles, body, 0, unroll=4)

    def collect(h, which, product):
        for n in range(8):
            par, e = blocks[n % 4]
            first = (2 * par + which) * width + origin(2 * h + n // 4, e) * piece
            at = pl.ds(pl.multiple_of(first, 16), piece)
            gram_ref[at, :] = gram_ref[at, :] + scale * product[n * piece : (n + 1) * piece]

    def swap(h):
        return remote(away.at[h], back.at[h], p_send.at[h], p_recv.at[h], sibling)

    def form(h):
        rows = width + (SIDE if h == 0 else 0)
        first = 0 if h == 0 else width + SIDE
        both = weighted[...].reshape(2 * width, total)
        product = lax.dot_general(design[first : first + rows], both, NT, preferred_element_type=f32)
        away[h] = product[:width, width:]
        swap(h).start()
        collect(h, core, product[:width, :width])
        if h == 0:
            rhs_ref[...] = rhs_prev_ref[...] + scale * jnp.sum(product[width : width + 8, :width], axis=0)

    def finish(h):
        swap(h).wait_recv()
        collect(h, 1 - core, back[h])

    def some(body, number, parts):
        lax.fori_loop(number * tiles // parts, (number + 1) * tiles // parts, body, 0, unroll=4)

    for copy in g1:
        copy.wait_recv()
    amount = part[row]
    for d in range(1, 8):
        amount = amount + land1[d]
    tot1[...] = amount
    g2 = [remote(tot1, land2.at[d], g2_send.at[d], g2_recv.at[d], far[d]) for d in range(1, nz)]
    for copy in g2:
        copy.start()

    for copy in s2:
        copy.wait_recv()
    turned[...] = samples[...].reshape(tile, 128).T
    for n in range(4):
        some(build_own, n, 4)
        if n == 1:
            for copy in g2:
                copy.wait_recv()
            amount = tot1[...]
            for d in range(1, nz):
                amount = amount + land2[d]
            sums[row] = amount
            g3 = [
                remote(sums.at[row], sums.at[row], g3_send.at[d], g3_recv.at[d], row_peers[d])
                for d in range(1, nrow)
            ]
            for copy in g3:
                copy.start()
        if n == 2:
            pass_y(0)
    pass_y(1)

    for copy in g3:
        copy.wait_recv()
    for a in range(2):
        for i in range(per):
            value = sums[a * per + i]
            for n in range(3):
                part_value = value.astype(bf16)
                pieces[a, n * MAXDEG : (n + 1) * MAXDEG, i * lanes : (i + 1) * lanes] = part_value
                value = value - part_value.astype(f32)
    build_rows(0)
    pass_on(0)

    residual = turned[3 * tiles : 4 * tiles, :] - pred[...]
    group = turned[5 * tiles : 6 * tiles, :]
    size = jnp.abs(residual)
    limit = jnp.zeros_like(size)
    for number in range(2):
        hot = (group == float(number)).astype(f32)
        count = jnp.sum(jnp.sum(hot, axis=0, keepdims=True), axis=1, keepdims=True)
        spread = jnp.sum(jnp.sum(hot * size, axis=0, keepdims=True), axis=1, keepdims=True)
        limit = limit + hot * (1.345 * spread / jnp.maximum(count, 1.0))
    turned[3 * tiles : 4 * tiles, :] = residual
    turned[5 * tiles : 6 * tiles, :] = limit / jnp.maximum(size, limit)
    some(weigh, 0, 1)
    w_copy = remote(weighted.at[0], weighted.at[1], w_send, w_recv, sibling)
    w_copy.start()

    pass_on(1)
    for par in range(2):
        for u in range(2):
            arrive(1, par, 1, u)
    build_rows(1)
    for par in range(2):
        for u in range(2):
            arrive(2, par, 0, u)
    build_rows(2)
    w_copy.wait_recv()
    prev_copy.wait()
    form(0)
    for par, e in blocks:
        for u in range(2):
            arrive(3, par, e, u)
    build_rows(3)
    finish(0)
    form(1)
    finish(1)

    for copy in s1 + s2 + g1 + g2 + g3 + zs + [w_copy]:
        copy.wait_send()
    for u in range(2):
        for d in range(nz):
            to = 2 * ((zhi + d) % nz) + y // 2
            for m in range(share):
                p = handed[d] * share + m
                target = zhi * 8 + 2 * (p // 2) + core

                @pl.when((to != row) | (target != col))
                def _():
                    here = own.at[p, u]
                    remote(here, here, x_send.at[d, m, u], x_recv.at[0, 0, u], (to, target)).wait_send()

        for par, e in blocks:
            for n in range(3):
                here = tab.at[n, par, e, u]
                remote(here, here, y_send.at[n, par, e, u], y_recv.at[0, par, e, u], right).wait_send()
    for h in range(2):
        swap(h).wait_send()


def local(nrow, ncol, sample_values, sample_codes, basis_tables, model_params, gram_prev, rhs_prev):
    ncell, width = basis_tables.shape[1:]
    lanes = 2 * ncell // nrow
    nz = ncol // 8
    tiles = sample_values.shape[1]
    tile = nrow * ncol
    total = tile * tiles
    piece = width // PIECES
    dma = pltpu.SemaphoreType.DMA
    vmem = pl.BlockSpec(memory_space=pltpu.VMEM)
    anywhere = pl.BlockSpec(memory_space=pl.ANY)
    f32, bf16 = jnp.float32, jnp.bfloat16
    return pl.pallas_call(
        functools.partial(kernel, nrow, ncol),
        out_shape=(
            pltpu.VMEM(gram_prev.shape, f32),
            pltpu.VMEM(rhs_prev.shape, f32),
        ),
        in_specs=[vmem, vmem, vmem, vmem, anywhere, vmem],
        out_specs=(vmem, vmem),
        scratch_shapes=[
            pltpu.VMEM((PIECES, 2, piece, ncell), bf16),
            pltpu.VMEM((4, 2, 2, 2, piece, ncell), bf16),
            pltpu.VMEM((nz, PIECES // nrow, 2, piece, ncell), bf16),
            pltpu.VMEM((nrow, MAXDEG, lanes), f32),
            pltpu.VMEM((8, MAXDEG, lanes), f32),
            pltpu.VMEM((MAXDEG, lanes), f32),
            pltpu.VMEM((nz, MAXDEG, lanes), f32),
            pltpu.VMEM((nrow, MAXDEG, lanes), f32),
            pltpu.VMEM((nrow, 1, 128), f32),
            pltpu.VMEM((ncol, nrow, 128), f32),
            pltpu.VMEM((128, tile), f32),
            pltpu.VMEM((2, 3 * MAXDEG, ncell), bf16),
            pltpu.VMEM((2, tiles, MAXDEG + piece, tile), f32),
            pltpu.VMEM((tiles, ncell, tile), bf16),
            pltpu.VMEM((tiles, tile), f32),
            pltpu.VMEM((2 * width + SIDE, total), bf16),
            pltpu.VMEM((2, width, total), bf16),
            pltpu.VMEM((2, width, width), f32),
            pltpu.VMEM((2, width, width), f32),
            dma((nrow,)), dma((nrow,)), dma((ncol,)), dma((ncol,)),
            dma((8,)), dma((8,)), dma((nz,)), dma((nz,)), dma((nrow,)), dma((nrow,)),
            dma((nz, PIECES // nrow, 2)), dma((nz, PIECES // nrow, 2)), dma((nz, PIECES // nrow, 2)),
            dma((2, 2, 2)), dma((3, 2, 2, 2)), dma((3, 2, 2, 2)),
            dma, dma, dma((2,)), dma((2,)), dma,
        ],
        compiler_params=pltpu.CompilerParams(
            collective_id=0, has_side_effects=True, vmem_limit_bytes=VMEM_LIMIT
        ),
    )(basis_tables, model_params, sample_values, sample_codes, gram_prev, rhs_prev)


def solution(mesh):
    placed = (
        P(None, ("row", "col")),
        P(None, ("row", "col")),
        P(None, None, "col"),
        P("col"),
        P("row", "col"),
        P("col"),
    )
    return jax.shard_map(
        functools.partial(local, mesh.shape["row"], mesh.shape["col"]),
        mesh=mesh,
        in_specs=placed,
        out_specs=(P("row", "col"), P("col")),
        check_vma=False,
    )
```

```python
import functools
import math

import jax
import jax.numpy as jnp
from jax import lax
from jax.experimental import pallas as pl
from jax.experimental.pallas import tpu as pltpu
from jax.sharding import PartitionSpec as P

MAXDEG = 64
MESH = pl.DeviceIdType.MESH
VMEM_LIMIT = 52 * 1024 * 1024
NT = (((1,), (1,)), ((), ()))
SIDE = 16
PARTS = ((0, 32), (32, 16))
PIECES = 8
UNROLL = 4


def kernel(
    nrow, ncol,
    basis_ref, params_ref, values_ref, codes_ref, prev_ref, rhs_prev_ref,
    gram_ref, rhs_ref,
    own, tab, zbuf, part, land1, tot1, land2, sums, slots, samples,
    turned, grown, hots, design, weighted, away, back,
    s1_send, s1_recv, s2_send, s2_recv,
    g1_send, g1_recv, g2_send, g2_recv, g3_send, g3_recv,
    z_send, z_recv, x_send, x_recv, y_send, y_recv,
    w_send, w_recv, p_send, p_recv, prev_sem,
):
    f32, bf16 = jnp.float32, jnp.bfloat16
    nz = ncol // 8
    row, col = lax.axis_index("row"), lax.axis_index("col")
    x, zlo = row // 2, row % 2
    zhi, yk = col // 8, col % 8
    y, core = yk // 2, yk % 2
    ncell, width = basis_ref.shape[1:]
    piece = width // PIECES
    share = PIECES // nrow
    quarter = 4 * piece
    tiles = values_ref.shape[1]
    tile = nrow * ncol
    total = tiles * tile
    mine = tiles // nrow
    scale = 1.0 / math.sqrt(total)

    def remote(src, dst, ssem, rsem, device):
        return pltpu.make_async_remote_copy(
            src_ref=src, dst_ref=dst, send_sem=ssem, recv_sem=rsem, device_id=device, device_id_type=MESH
        )

    left = (row, zhi * 8 + 2 * ((y + 3) % 4) + core)
    right = (row, zhi * 8 + 2 * ((y + 1) % 4) + core)
    sibling = (row, zhi * 8 + 2 * y + 1 - core)
    col_peers = [(row, (col + d) % ncol) for d in range(ncol)]
    row_peers = [((row + d) % nrow, col) for d in range(nrow)]
    near = [(row, zhi * 8 + (yk + d) % 8) for d in range(8)]
    far = [(row, ((zhi + d) % nz) * 8 + yk) for d in range(nz)]
    other = row + 1 - 2 * zlo
    hand = [(other, far[d][1]) if 2 * d == nz else far[d] for d in range(nz)]
    handed = [other if 2 * d == nz else row for d in range(nz)]
    parity = y % 2
    blocks = [(par, e) for par in range(2) for e in range(2)]
    offsets = (0, 3, 1, 2)

    barrier = pltpu.get_barrier_semaphore()
    greeted = col_peers[1:] + row_peers[1:] + [hand[d] for d in range(1, nz) if 2 * d == nz]
    for peer in greeted:
        pl.semaphore_signal(barrier, inc=1, device_id=peer, device_id_type=MESH)

    selves = 0
    for par, e in blocks:
        giver = (2 * y + e) // share
        if nz > 1:
            giver = jnp.where(2 * ((x - zhi + nz) % nz) == nz, giver + 1 - 2 * (giver % 2), giver)
        place = zhi * 8 + 2 * (2 * zlo + par) + core
        to_self = (giver == row) & (place == col)
        selves = selves + to_self.astype(jnp.int32)

        @pl.when(jnp.logical_not(to_self))
        def _():
            pl.semaphore_signal(barrier, inc=1, device_id=(giver, place), device_id_type=MESH)

    prev_copy = pltpu.make_async_copy(prev_ref, gram_ref, prev_sem)
    prev_copy.start()

    slots[row] = jnp.concatenate(
        [values_ref[i : i + 1, :] for i in range(4)]
        + [codes_ref[i : i + 1, :].astype(f32) for i in range(2)]
        + [jnp.zeros((1, 128 - 6 * tiles), f32)],
        axis=1,
    )
    for a in range(2):
        whole = jnp.concatenate(
            [basis_ref[a, :, 128 * j : 128 * (j + 1)].astype(f32).T for j in range(width // 128)], axis=0
        ).astype(bf16)
        for p in range(PIECES):
            for begin, rows in PARTS:
                own[p, 2 * begin + a * rows : 2 * begin + (a + 1) * rows] = whole[
                    piece * p + begin : piece * p + begin + rows
                ]

    pl.semaphore_wait(barrier, len(greeted) + len(blocks) - selves)

    s1 = [remote(slots.at[row], slots.at[row], s1_send.at[d], s1_recv.at[d], row_peers[d]) for d in range(1, nrow)]
    for copy in s1:
        copy.start()

    def half(ref, u):
        begin, rows = PARTS[u]
        return ref.at[pl.ds(2 * begin, 2 * rows)]

    def pass_z(d, u):
        return [
            remote(half(own.at[row * share + m], u), half(zbuf.at[nz - d, m], u), z_send.at[d, m, u], z_recv.at[nz - d, m, u], hand[d])
            for m in range(share)
        ]

    def pass_x(d, u):
        to = 2 * ((zhi + d) % nz) + y // 2
        for m in range(share):
            p = handed[d] * share + m
            target = zhi * 8 + 2 * (p // 2) + core
            source = half(own.at[p] if d == 0 else zbuf.at[d, m], u)
            place = half(tab.at[0, parity, p % 2], u)
            arrived = x_recv.at[parity, p % 2, u]
            to_self = (to == row) & (target == col)

            @pl.when(jnp.logical_not(to_self))
            def _():
                remote(source, place, x_send.at[d, m, u], arrived, (to, target)).start()

            @pl.when(to_self)
            def _():
                pltpu.make_async_copy(source, place, arrived).start()

    zs = [[copy for d in range(1, nz) for copy in pass_z(d, u)] for u in range(2)]
    for copy in zs[0]:
        copy.start()
    for u in range(2):
        pass_x(0, u)

    rest = params_ref[...].reshape(1, width)
    terms = []
    for n in range(3):
        terms.append(rest.astype(bf16).astype(f32))
        rest = rest - terms[-1]
    terms = jnp.concatenate(terms + [jnp.zeros((SIDE - 3, width), f32)], axis=0).astype(bf16)

    for copy in s1:
        copy.wait_recv()
    for i in range(nrow):
        samples[col, pl.ds(i, 1)] = slots[i]
    s2 = [
        remote(samples.at[col], samples.at[col], s2_send.at[d], s2_recv.at[d], col_peers[d]) for d in range(1, ncol)
    ]
    for copy in s2:
        copy.start()
    for copy in zs[1]:
        copy.start()

    def pass_zx(u):
        for d in range(1, nz):
            for m in range(share):
                here = half(zbuf.at[d, m], u)
                remote(here, here, z_send.at[d, m, u], z_recv.at[d, m, u], hand[d]).wait_recv()
            pass_x(d, u)

    def pass_y(u):
        for par, e in blocks:
            here = half(tab.at[0, par, e], u)
            pltpu.make_async_copy(here, here, x_recv.at[par, e, u]).wait()
            remote(here, half(tab.at[1, par, e], u), y_send.at[0, par, e, u], y_recv.at[0, par, e, u], right).start()
            remote(here, half(tab.at[2, par, e], u), y_send.at[1, par, e, u], y_recv.at[1, par, e, u], left).start()

    def arrive(g, par, e, u):
        here = half(tab.at[g, par, e], u)
        remote(here, here, y_send.at[0, par, e, u], y_recv.at[g - 1, par, e, u], right).wait_recv()

    def pass_on(u):
        for par in range(2):
            for g, to in ((1, right), (2, left)):
                e = g - 1
                arrive(g, par, e, u)
                remote(
                    half(tab.at[g, par, e], u), half(tab.at[3, par, e], u), y_send.at[2, par, e, u], y_recv.at[2, par, e, u], to
                ).start()

    def field(number, k):
        return turned[pl.ds(number * tiles + k, 1), :]

    def span(k):
        return pl.ds(pl.multiple_of(k * tile, tile), tile)

    exponent = (lax.broadcasted_iota(jnp.int32, (MAXDEG, tile), 0) + 1).astype(f32)
    cells = lax.broadcasted_iota(jnp.int32, (ncell, tile), 0).astype(jnp.int16)
    reach = grown.shape[2]

    def build_own(number, carry):
        k = (number + row * mine) % tiles
        hot = jnp.where(cells == field(4, k).astype(jnp.int32).astype(jnp.int16), jnp.bfloat16(1), jnp.bfloat16(0))
        hots[k] = hot
        grow = jnp.exp(field(2, k) * exponent)
        grows = []
        for a in range(2):
            value = grow * field(a, k)
            value = jnp.concatenate([value, value], axis=0)
            grown[a, k] = value[:reach]
            grows.append(value)
        picked = jnp.dot(own[...].reshape(2 * width, ncell), hot, preferred_element_type=f32)
        for p in range(PIECES):
            for begin, rows in PARTS:
                first = 2 * (piece * p + begin)
                at = (p * piece + begin) % MAXDEG
                weighted[0, p * piece + begin : p * piece + begin + rows, span(k)] = (
                    picked[first : first + rows] * grows[0][at : at + rows]
                    + picked[first + rows : first + 2 * rows] * grows[1][at : at + rows]
                ).astype(bf16)
        return carry

    def mixed(picked, k, begin, rows):
        at = pl.ds(pl.multiple_of(begin % MAXDEG, 16), rows)
        return (picked[:rows] * grown[0, k, at] + picked[rows:] * grown[1, k, at]).astype(bf16)

    def weigh(k, carry):
        weighted[0, :, span(k)] = (weighted[0, :, span(k)].astype(f32) * field(5, k)).astype(bf16)
        rest = field(3, k)
        split = []
        for n in range(3):
            split.append(rest.astype(bf16).astype(f32))
            rest = rest - split[-1]
        split.append(jnp.zeros((SIDE - 3, tile), f32))
        design[3 * quarter : 3 * quarter + SIDE, span(k)] = jnp.concatenate(split, axis=0).astype(bf16)
        return carry

    def origin(g, e):
        return 2 * ((y + offsets[g]) % 4) + e

    def first_row(g):
        return g * quarter + (SIDE if g > 2 else 0)

    def build_rows(groups, parts):
        lo = PARTS[parts[0]][0]
        hi = sum(PARTS[parts[-1]])
        size = 2 * (hi - lo)

        def body(k, carry):
            lhs = tab[groups[0] : groups[-1] + 1, :, :, 2 * lo : 2 * hi].reshape(4 * size * len(groups), ncell)
            picked = jnp.dot(lhs, hots[k], preferred_element_type=f32)
            for j, g in enumerate(groups):
                for n, (par, e) in enumerate(blocks):
                    for u in parts:
                        begin, rows = PARTS[u]
                        at = first_row(g) + n * piece + begin
                        first = size * (4 * j + n) + 2 * (begin - lo)
                        design[at : at + rows, span(k)] = mixed(
                            picked[first : first + 2 * rows], k, origin(g, e) * piece + begin, rows
                        )
            return carry

        lax.fori_loop(0, tiles, body, 0, unroll=UNROLL)

    def collect(groups, which, product):
        for j, g in enumerate(groups):
            for n, (par, e) in enumerate(blocks):
                at = pl.ds(pl.multiple_of((2 * par + which) * width + origin(g, e) * piece, 16), piece)
                begin = j * quarter + n * piece
                gram_ref[at, :] = gram_ref[at, :] + scale * product[begin : begin + piece]

    def swap(groups):
        at, g = pl.ds(groups[0] * quarter, len(groups) * quarter), groups[0]
        return remote(away.at[at], back.at[at], p_send.at[g], p_recv.at[g], sibling)

    def form(groups):
        count = len(groups) * quarter
        rows = count + (SIDE if groups[0] == 0 else 0)
        first = first_row(groups[0])
        both = weighted[...].reshape(2 * width, total)
        product = lax.dot_general(design[first : first + rows], both, NT, preferred_element_type=f32)
        away[groups[0] * quarter : groups[0] * quarter + count] = product[:count, width:]
        swap(groups).start()
        collect(groups, core, product[:count, :width])
        if groups[0] == 0:
            rhs_ref[...] = rhs_prev_ref[...] + scale * jnp.sum(product[count : count + 8, :width], axis=0)

    def finish(groups):
        swap(groups).wait_recv()
        collect(groups, 1 - core, back[groups[0] * quarter : (groups[-1] + 1) * quarter])

    def some(body, number, parts):
        lax.fori_loop(number * tiles // parts, (number + 1) * tiles // parts, body, 0, unroll=UNROLL)

    pass_zx(0)
    for copy in s2:
        copy.wait_recv()
    turned[...] = samples[...].reshape(tile, 128).T
    some(build_own, 0, 4)
    early = -(-4 * mine // tiles)
    for n in range(1, early):
        some(build_own, n, 4)
    for j in range(mine):
        value = jnp.dot(terms, weighted[0, :, span(row * mine + j)], preferred_element_type=f32)
        part[j : j + 1, :] = jnp.sum(value[:8], axis=0, keepdims=True)
    g1 = [remote(part, land1.at[d], g1_send.at[d], g1_recv.at[d], near[d]) for d in range(1, 8)]
    for copy in g1:
        copy.start()
    for n in range(early, 2):
        some(build_own, n, 4)
    pass_zx(1)
    some(build_own, 2, 4)
    for copy in g1:
        copy.wait_recv()
    amount = part[...]
    for d in range(1, 8):
        amount = amount + land1[d]
    tot1[...] = amount
    g2 = [remote(tot1, land2.at[d], g2_send.at[d], g2_recv.at[d], far[d]) for d in range(1, nz)]
    for copy in g2:
        copy.start()
    some(build_own, 3, 4)
    pass_y(0)
    for copy in g2:
        copy.wait_recv()
    amount = tot1[...]
    for d in range(1, nz):
        amount = amount + land2[d]
    sums[row] = amount
    g3 = [remote(sums.at[row], sums.at[row], g3_send.at[d], g3_recv.at[d], row_peers[d]) for d in range(1, nrow)]
    for copy in g3:
        copy.start()
    pass_y(1)
    build_rows((0,), (0, 1))
    pass_on(0)
    for copy in g3:
        copy.wait_recv()

    residual = turned[3 * tiles : 4 * tiles, :] - jnp.concatenate([sums[r] for r in range(nrow)], axis=0)
    group = turned[5 * tiles : 6 * tiles, :]
    size = jnp.abs(residual)
    limit = jnp.zeros_like(size)
    for number in range(2):
        hot = (group == float(number)).astype(f32)
        count = jnp.sum(jnp.sum(hot, axis=0, keepdims=True), axis=1, keepdims=True)
        spread = jnp.sum(jnp.sum(hot * size, axis=0, keepdims=True), axis=1, keepdims=True)
        limit = limit + hot * (1.345 * spread / jnp.maximum(count, 1.0))
    turned[3 * tiles : 4 * tiles, :] = residual
    turned[5 * tiles : 6 * tiles, :] = limit / jnp.maximum(size, limit)
    some(weigh, 0, 1)
    w_copy = remote(weighted.at[0], weighted.at[1], w_send, w_recv, sibling)
    w_copy.start()

    for par in range(2):
        arrive(1, par, 1, 0)
        arrive(2, par, 0, 0)
    build_rows((1, 2), (0,))
    pass_on(1)
    for par in range(2):
        arrive(1, par, 1, 1)
        arrive(2, par, 0, 1)
    build_rows((1, 2), (1,))
    w_copy.wait_recv()
    prev_copy.wait()
    form((0, 1, 2))
    for par, e in blocks:
        for u in range(2):
            arrive(3, par, e, u)
    build_rows((3,), (0, 1))
    form((3,))
    finish((0, 1, 2))
    finish((3,))

    for copy in s1 + s2 + g1 + g2 + g3 + zs[0] + zs[1] + [w_copy]:
        copy.wait_send()
    for u in range(2):
        for d in range(nz):
            to = 2 * ((zhi + d) % nz) + y // 2
            for m in range(share):
                p = handed[d] * share + m
                target = zhi * 8 + 2 * (p // 2) + core

                @pl.when((to != row) | (target != col))
                def _():
                    here = half(own.at[p], u)
                    remote(here, here, x_send.at[d, m, u], x_recv.at[0, 0, u], (to, target)).wait_send()

        for par, e in blocks:
            for n in range(3):
                here = half(tab.at[n, par, e], u)
                remote(here, here, y_send.at[n, par, e, u], y_recv.at[0, par, e, u], right).wait_send()
    for groups in ((0, 1, 2), (3,)):
        swap(groups).wait_send()


def local(nrow, ncol, sample_values, sample_codes, basis_tables, model_params, gram_prev, rhs_prev):
    ncell, width = basis_tables.shape[1:]
    nz = ncol // 8
    tiles = sample_values.shape[1]
    tile = nrow * ncol
    total = tile * tiles
    piece = width // PIECES
    dma = pltpu.SemaphoreType.DMA
    vmem = pl.BlockSpec(memory_space=pltpu.VMEM)
    anywhere = pl.BlockSpec(memory_space=pl.ANY)
    f32, bf16 = jnp.float32, jnp.bfloat16
    return pl.pallas_call(
        functools.partial(kernel, nrow, ncol),
        out_shape=(
            pltpu.VMEM(gram_prev.shape, f32),
            pltpu.VMEM(rhs_prev.shape, f32),
        ),
        in_specs=[vmem, vmem, vmem, vmem, anywhere, vmem],
        out_specs=(vmem, vmem),
        scratch_shapes=[
            pltpu.VMEM((PIECES, 2 * piece, ncell), bf16),
            pltpu.VMEM((4, 2, 2, 2 * piece, ncell), bf16),
            pltpu.VMEM((nz, PIECES // nrow, 2 * piece, ncell), bf16),
            pltpu.VMEM((tiles // nrow, tile), f32),
            pltpu.VMEM((8, tiles // nrow, tile), f32),
            pltpu.VMEM((tiles // nrow, tile), f32),
            pltpu.VMEM((nz, tiles // nrow, tile), f32),
            pltpu.VMEM((nrow, tiles // nrow, tile), f32),
            pltpu.VMEM((nrow, 1, 128), f32),
            pltpu.VMEM((ncol, nrow, 128), f32),
            pltpu.VMEM((128, tile), f32),
            pltpu.VMEM((2, tiles, MAXDEG + piece, tile), f32),
            pltpu.VMEM((tiles, ncell, tile), bf16),
            pltpu.VMEM((2 * width + SIDE, total), bf16),
            pltpu.VMEM((2, width, total), bf16),
            pltpu.VMEM((2 * width, width), f32),
            pltpu.VMEM((2 * width, width), f32),
            dma((nrow,)), dma((nrow,)), dma((ncol,)), dma((ncol,)),
            dma((8,)), dma((8,)), dma((nz,)), dma((nz,)), dma((nrow,)), dma((nrow,)),
            dma((nz, PIECES // nrow, 2)), dma((nz, PIECES // nrow, 2)), dma((nz, PIECES // nrow, 2)),
            dma((2, 2, 2)), dma((3, 2, 2, 2)), dma((3, 2, 2, 2)),
            dma, dma, dma((4,)), dma((4,)), dma,
        ],
        compiler_params=pltpu.CompilerParams(
            collective_id=0, has_side_effects=True, vmem_limit_bytes=VMEM_LIMIT
        ),
    )(basis_tables, model_params, sample_values, sample_codes, gram_prev, rhs_prev)


def solution(mesh):
    placed = (
        P(None, ("row", "col")),
        P(None, ("row", "col")),
        P(None, None, "col"),
        P("col"),
        P("row", "col"),
        P("col"),
    )
    return jax.shard_map(
        functools.partial(local, mesh.shape["row"], mesh.shape["col"]),
        mesh=mesh,
        in_specs=placed,
        out_specs=(P("row", "col"), P("col")),
        check_vma=False,
    )
```

```python
import functools
import math

import jax
import jax.numpy as jnp
from jax import lax
from jax.experimental import pallas as pl
from jax.experimental.pallas import tpu as pltpu
from jax.sharding import PartitionSpec as P

MAXDEG = 64
MESH = pl.DeviceIdType.MESH
VMEM_LIMIT = 52 * 1024 * 1024
NT = (((1,), (1,)), ((), ()))
SIDE = 16
PARTS = ((0, 32), (32, 16))
PIECES = 8
UNROLL = 4


def kernel(
    nrow, ncol,
    basis_ref, params_ref, values_ref, codes_ref, prev_ref, rhs_prev_ref,
    gram_ref, rhs_ref,
    own, tab, zbuf, part, land1, tot1, land2, sums, slots, samples,
    turned, grown, hots, design, weighted, away, back,
    s1_send, s1_recv, s2_send, s2_recv,
    g1_send, g1_recv, g2_send, g2_recv, g3_send, g3_recv,
    z_send, z_recv, x_send, x_recv, y_send, y_recv,
    w_send, w_recv, p_send, p_recv, prev_sem,
):
    f32, bf16 = jnp.float32, jnp.bfloat16
    nz = ncol // 8
    row, col = lax.axis_index("row"), lax.axis_index("col")
    x, zlo = row // 2, row % 2
    zhi, yk = col // 8, col % 8
    y, core = yk // 2, yk % 2
    ncell, width = basis_ref.shape[1:]
    piece = width // PIECES
    share = PIECES // nrow
    quarter = 4 * piece
    tiles = values_ref.shape[1]
    tile = nrow * ncol
    total = tiles * tile
    mine = tiles // nrow
    scale = 1.0 / math.sqrt(total)

    def remote(src, dst, ssem, rsem, device):
        return pltpu.make_async_remote_copy(
            src_ref=src, dst_ref=dst, send_sem=ssem, recv_sem=rsem, device_id=device, device_id_type=MESH
        )

    left = (row, zhi * 8 + 2 * ((y + 3) % 4) + core)
    right = (row, zhi * 8 + 2 * ((y + 1) % 4) + core)
    sibling = (row, zhi * 8 + 2 * y + 1 - core)
    col_peers = [(row, (col + d) % ncol) for d in range(ncol)]
    row_peers = [((row + d) % nrow, col) for d in range(nrow)]
    near = [(row, zhi * 8 + (yk + d) % 8) for d in range(8)]
    far = [(row, ((zhi + d) % nz) * 8 + yk) for d in range(nz)]
    other = row + 1 - 2 * zlo
    hand = [(other, far[d][1]) if 2 * d == nz else far[d] for d in range(nz)]
    handed = [other if 2 * d == nz else row for d in range(nz)]
    parity = y % 2
    blocks = [(par, e) for par in range(2) for e in range(2)]
    offsets = (0, 3, 1, 2)

    barrier = pltpu.get_barrier_semaphore()
    greeted = col_peers[1:] + row_peers[1:] + [hand[d] for d in range(1, nz) if 2 * d == nz]
    for peer in greeted:
        pl.semaphore_signal(barrier, inc=1, device_id=peer, device_id_type=MESH)

    selves = 0
    for par, e in blocks:
        giver = (2 * y + e) // share
        if nz > 1:
            giver = jnp.where(2 * ((x - zhi + nz) % nz) == nz, giver + 1 - 2 * (giver % 2), giver)
        place = zhi * 8 + 2 * (2 * zlo + par) + core
        to_self = (giver == row) & (place == col)
        selves = selves + to_self.astype(jnp.int32)

        @pl.when(jnp.logical_not(to_self))
        def _():
            pl.semaphore_signal(barrier, inc=1, device_id=(giver, place), device_id_type=MESH)

    prev_copy = pltpu.make_async_copy(prev_ref, gram_ref, prev_sem)
    prev_copy.start()

    slots[row] = jnp.concatenate(
        [values_ref[i : i + 1, :] for i in range(4)]
        + [codes_ref[i : i + 1, :].astype(f32) for i in range(2)]
        + [jnp.zeros((1, 128 - 6 * tiles), f32)],
        axis=1,
    )
    for a in range(2):
        whole = jnp.concatenate(
            [basis_ref[a, :, 128 * j : 128 * (j + 1)].astype(f32).T for j in range(width // 128)], axis=0
        ).astype(bf16)
        for p in range(PIECES):
            for begin, rows in PARTS:
                own[p, 2 * begin + a * rows : 2 * begin + (a + 1) * rows] = whole[
                    piece * p + begin : piece * p + begin + rows
                ]

    pl.semaphore_wait(barrier, len(greeted) + len(blocks) - selves)

    s1 = [remote(slots.at[row], slots.at[row], s1_send.at[d], s1_recv.at[d], row_peers[d]) for d in range(1, nrow)]
    for copy in s1:
        copy.start()

    def half(ref, u):
        begin, rows = PARTS[u]
        return ref.at[pl.ds(2 * begin, 2 * rows)]

    def pass_z(d, u):
        return [
            remote(half(own.at[row * share + m], u), half(zbuf.at[nz - d, m], u), z_send.at[d, m, u], z_recv.at[nz - d, m, u], hand[d])
            for m in range(share)
        ]

    def pass_x(d, u):
        to = 2 * ((zhi + d) % nz) + y // 2
        for m in range(share):
            p = handed[d] * share + m
            target = zhi * 8 + 2 * (p // 2) + core
            source = half(own.at[p] if d == 0 else zbuf.at[d, m], u)
            place = half(tab.at[0, parity, p % 2], u)
            arrived = x_recv.at[parity, p % 2, u]
            to_self = (to == row) & (target == col)

            @pl.when(jnp.logical_not(to_self))
            def _():
                remote(source, place, x_send.at[d, m, u], arrived, (to, target)).start()

            @pl.when(to_self)
            def _():
                pltpu.make_async_copy(source, place, arrived).start()

    zs = [[copy for d in range(1, nz) for copy in pass_z(d, u)] for u in range(2)]
    for copy in zs[0]:
        copy.start()
    for u in range(2):
        pass_x(0, u)

    rest = params_ref[...].reshape(1, width)
    terms = []
    for n in range(3):
        terms.append(rest.astype(bf16).astype(f32))
        rest = rest - terms[-1]
    terms = jnp.concatenate(terms + [jnp.zeros((SIDE - 3, width), f32)], axis=0).astype(bf16)

    for copy in s1:
        copy.wait_recv()
    for i in range(nrow):
        samples[col, pl.ds(i, 1)] = slots[i]
    s2 = [
        remote(samples.at[col], samples.at[col], s2_send.at[d], s2_recv.at[d], col_peers[d]) for d in range(1, ncol)
    ]
    for copy in s2:
        copy.start()
    for copy in zs[1]:
        copy.start()

    def pass_zx(u):
        for d in range(1, nz):
            for m in range(share):
                here = half(zbuf.at[d, m], u)
                remote(here, here, z_send.at[d, m, u], z_recv.at[d, m, u], hand[d]).wait_recv()
            pass_x(d, u)

    def pass_y(u):
        for par, e in blocks:
            here = half(tab.at[0, par, e], u)
            pltpu.make_async_copy(here, here, x_recv.at[par, e, u]).wait()
            remote(here, half(tab.at[1, par, e], u), y_send.at[0, par, e, u], y_recv.at[0, par, e, u], right).start()
            remote(here, half(tab.at[2, par, e], u), y_send.at[1, par, e, u], y_recv.at[1, par, e, u], left).start()

    def arrive(g, par, e, u):
        here = half(tab.at[g, par, e], u)
        remote(here, here, y_send.at[0, par, e, u], y_recv.at[g - 1, par, e, u], right).wait_recv()

    def pass_on(u):
        for par in range(2):
            for g, to in ((1, right), (2, left)):
                e = g - 1
                arrive(g, par, e, u)
                remote(
                    half(tab.at[g, par, e], u), half(tab.at[3, par, e], u), y_send.at[2, par, e, u], y_recv.at[2, par, e, u], to
                ).start()

    def field(number, k):
        return turned[pl.ds(number * tiles + k, 1), :]

    def span(k):
        return pl.ds(pl.multiple_of(k * tile, tile), tile)

    exponent = (lax.broadcasted_iota(jnp.int32, (MAXDEG, tile), 0) + 1).astype(f32)
    cells = lax.broadcasted_iota(jnp.int32, (ncell, tile), 0).astype(jnp.int16)
    reach = grown.shape[2]

    def build_own(number, carry):
        k = (number + row * mine) % tiles
        hot = jnp.where(cells == field(4, k).astype(jnp.int32).astype(jnp.int16), jnp.bfloat16(1), jnp.bfloat16(0))
        hots[k] = hot
        grow = jnp.exp(field(2, k) * exponent)
        grows = []
        for a in range(2):
            value = grow * field(a, k)
            value = jnp.concatenate([value, value], axis=0)
            grown[a, k] = value[:reach]
            grows.append(value)
        picked = jnp.dot(own[...].reshape(2 * width, ncell), hot, preferred_element_type=f32)
        for p in range(PIECES):
            for begin, rows in PARTS:
                first = 2 * (piece * p + begin)
                at = (p * piece + begin) % MAXDEG
                weighted[0, p * piece + begin : p * piece + begin + rows, span(k)] = (
                    picked[first : first + rows] * grows[0][at : at + rows]
                    + picked[first + rows : first + 2 * rows] * grows[1][at : at + rows]
                ).astype(bf16)
        return carry

    def mixed(picked, k, begin, rows):
        at = pl.ds(pl.multiple_of(begin % MAXDEG, 16), rows)
        return (picked[:rows] * grown[0, k, at] + picked[rows:] * grown[1, k, at]).astype(bf16)

    def weigh(k, carry):
        weighted[0, :, span(k)] = (weighted[0, :, span(k)].astype(f32) * field(5, k)).astype(bf16)
        rest = field(3, k)
        split = []
        for n in range(3):
            split.append(rest.astype(bf16).astype(f32))
            rest = rest - split[-1]
        split.append(jnp.zeros((SIDE - 3, tile), f32))
        design[3 * quarter : 3 * quarter + SIDE, span(k)] = jnp.concatenate(split, axis=0).astype(bf16)
        return carry

    def origin(g, e):
        return 2 * ((y + offsets[g]) % 4) + e

    def first_row(g):
        return g * quarter + (SIDE if g > 2 else 0)

    def build_rows(groups, parts):
        lo = PARTS[parts[0]][0]
        hi = sum(PARTS[parts[-1]])
        size = 2 * (hi - lo)

        def body(k, carry):
            lhs = tab[groups[0] : groups[-1] + 1, :, :, 2 * lo : 2 * hi].reshape(4 * size * len(groups), ncell)
            picked = jnp.dot(lhs, hots[k], preferred_element_type=f32)
            for j, g in enumerate(groups):
                for n, (par, e) in enumerate(blocks):
                    for u in parts:
                        begin, rows = PARTS[u]
                        at = first_row(g) + n * piece + begin
                        first = size * (4 * j + n) + 2 * (begin - lo)
                        design[at : at + rows, span(k)] = mixed(
                            picked[first : first + 2 * rows], k, origin(g, e) * piece + begin, rows
                        )
            return carry

        lax.fori_loop(0, tiles, body, 0, unroll=UNROLL)

    def collect(groups, which, product):
        for j, g in enumerate(groups):
            for n, (par, e) in enumerate(blocks):
                at = pl.ds(pl.multiple_of((2 * par + which) * width + origin(g, e) * piece, 16), piece)
                begin = j * quarter + n * piece
                gram_ref[at, :] = gram_ref[at, :] + scale * product[begin : begin + piece]

    def swap(groups):
        at, g = pl.ds(groups[0] * quarter, len(groups) * quarter), groups[0]
        return remote(away.at[at], back.at[at], p_send.at[g], p_recv.at[g], sibling)

    def form(groups):
        count = len(groups) * quarter
        rows = count + (SIDE if groups[0] == 0 else 0)
        first = first_row(groups[0])
        if groups[-1] == 3:
            lhs = design[first : first + rows]
            away[groups[0] * quarter : groups[0] * quarter + count] = lax.dot_general(
                lhs, weighted[1], NT, preferred_element_type=f32
            )
            swap(groups).start()
            collect(groups, core, lax.dot_general(lhs, weighted[0], NT, preferred_element_type=f32))
            return
        both = weighted[...].reshape(2 * width, total)
        product = lax.dot_general(design[first : first + rows], both, NT, preferred_element_type=f32)
        away[groups[0] * quarter : groups[0] * quarter + count] = product[:count, width:]
        swap(groups).start()
        collect(groups, core, product[:count, :width])
        if groups[0] == 0:
            rhs_ref[...] = rhs_prev_ref[...] + scale * jnp.sum(product[count : count + 8, :width], axis=0)

    def finish(groups):
        swap(groups).wait_recv()
        collect(groups, 1 - core, back[groups[0] * quarter : (groups[-1] + 1) * quarter])

    def some(body, number, parts):
        lax.fori_loop(number * tiles // parts, (number + 1) * tiles // parts, body, 0, unroll=UNROLL)

    pass_zx(0)
    for copy in s2:
        copy.wait_recv()
    turned[...] = samples[...].reshape(tile, 128).T
    some(build_own, 0, 4)
    early = -(-4 * mine // tiles)
    for n in range(1, early):
        some(build_own, n, 4)
    for j in range(mine):
        value = jnp.dot(terms, weighted[0, :, span(row * mine + j)], preferred_element_type=f32)
        part[j : j + 1, :] = jnp.sum(value[:8], axis=0, keepdims=True)
    g1 = [remote(part, land1.at[d], g1_send.at[d], g1_recv.at[d], near[d]) for d in range(1, 8)]
    for copy in g1:
        copy.start()
    for n in range(early, 2):
        some(build_own, n, 4)
    pass_zx(1)
    some(build_own, 2, 4)
    for copy in g1:
        copy.wait_recv()
    amount = part[...]
    for d in range(1, 8):
        amount = amount + land1[d]
    tot1[...] = amount
    g2 = [remote(tot1, land2.at[d], g2_send.at[d], g2_recv.at[d], far[d]) for d in range(1, nz)]
    for copy in g2:
        copy.start()
    some(build_own, 3, 4)
    pass_y(0)
    build_rows((0,), (0,))
    for copy in g2:
        copy.wait_recv()
    amount = tot1[...]
    for d in range(1, nz):
        amount = amount + land2[d]
    sums[row] = amount
    g3 = [remote(sums.at[row], sums.at[row], g3_send.at[d], g3_recv.at[d], row_peers[d]) for d in range(1, nrow)]
    for copy in g3:
        copy.start()
    pass_y(1)
    build_rows((0,), (1,))
    pass_on(0)
    for copy in g3:
        copy.wait_recv()

    residual = turned[3 * tiles : 4 * tiles, :] - jnp.concatenate([sums[r] for r in range(nrow)], axis=0)
    group = turned[5 * tiles : 6 * tiles, :]
    size = jnp.abs(residual)
    limit = jnp.zeros_like(size)
    for number in range(2):
        hot = (group == float(number)).astype(f32)
        count = jnp.sum(jnp.sum(hot, axis=0, keepdims=True), axis=1, keepdims=True)
        spread = jnp.sum(jnp.sum(hot * size, axis=0, keepdims=True), axis=1, keepdims=True)
        limit = limit + hot * (1.345 * spread / jnp.maximum(count, 1.0))
    turned[3 * tiles : 4 * tiles, :] = residual
    turned[5 * tiles : 6 * tiles, :] = limit / jnp.maximum(size, limit)
    some(weigh, 0, 1)
    w_copy = remote(weighted.at[0], weighted.at[1], w_send, w_recv, sibling)
    w_copy.start()

    for par in range(2):
        arrive(1, par, 1, 0)
        arrive(2, par, 0, 0)
    build_rows((1, 2), (0,))
    pass_on(1)
    for par in range(2):
        arrive(1, par, 1, 1)
        arrive(2, par, 0, 1)
    build_rows((1, 2), (1,))
    w_copy.wait_recv()
    prev_copy.wait()
    form((0, 1, 2))
    for par, e in blocks:
        for u in range(2):
            arrive(3, par, e, u)
    build_rows((3,), (0, 1))
    form((3,))
    finish((0, 1, 2))
    finish((3,))

    for copy in s1 + s2 + g1 + g2 + g3 + zs[0] + zs[1] + [w_copy]:
        copy.wait_send()
    for u in range(2):
        for d in range(nz):
            to = 2 * ((zhi + d) % nz) + y // 2
            for m in range(share):
                p = handed[d] * share + m
                target = zhi * 8 + 2 * (p // 2) + core

                @pl.when((to != row) | (target != col))
                def _():
                    here = half(own.at[p], u)
                    remote(here, here, x_send.at[d, m, u], x_recv.at[0, 0, u], (to, target)).wait_send()

        for par, e in blocks:
            for n in range(3):
                here = half(tab.at[n, par, e], u)
                remote(here, here, y_send.at[n, par, e, u], y_recv.at[0, par, e, u], right).wait_send()
    for groups in ((0, 1, 2), (3,)):
        swap(groups).wait_send()


def local(nrow, ncol, sample_values, sample_codes, basis_tables, model_params, gram_prev, rhs_prev):
    ncell, width = basis_tables.shape[1:]
    nz = ncol // 8
    tiles = sample_values.shape[1]
    tile = nrow * ncol
    total = tile * tiles
    piece = width // PIECES
    dma = pltpu.SemaphoreType.DMA
    vmem = pl.BlockSpec(memory_space=pltpu.VMEM)
    anywhere = pl.BlockSpec(memory_space=pl.ANY)
    f32, bf16 = jnp.float32, jnp.bfloat16
    return pl.pallas_call(
        functools.partial(kernel, nrow, ncol),
        out_shape=(
            pltpu.VMEM(gram_prev.shape, f32),
            pltpu.VMEM(rhs_prev.shape, f32),
        ),
        in_specs=[vmem, vmem, vmem, vmem, anywhere, vmem],
        out_specs=(vmem, vmem),
        scratch_shapes=[
            pltpu.VMEM((PIECES, 2 * piece, ncell), bf16),
            pltpu.VMEM((4, 2, 2, 2 * piece, ncell), bf16),
            pltpu.VMEM((nz, PIECES // nrow, 2 * piece, ncell), bf16),
            pltpu.VMEM((tiles // nrow, tile), f32),
            pltpu.VMEM((8, tiles // nrow, tile), f32),
            pltpu.VMEM((tiles // nrow, tile), f32),
            pltpu.VMEM((nz, tiles // nrow, tile), f32),
            pltpu.VMEM((nrow, tiles // nrow, tile), f32),
            pltpu.VMEM((nrow, 1, 128), f32),
            pltpu.VMEM((ncol, nrow, 128), f32),
            pltpu.VMEM((128, tile), f32),
            pltpu.VMEM((2, tiles, MAXDEG + piece, tile), f32),
            pltpu.VMEM((tiles, ncell, tile), bf16),
            pltpu.VMEM((2 * width + SIDE, total), bf16),
            pltpu.VMEM((2, width, total), bf16),
            pltpu.VMEM((2 * width, width), f32),
            pltpu.VMEM((2 * width, width), f32),
            dma((nrow,)), dma((nrow,)), dma((ncol,)), dma((ncol,)),
            dma((8,)), dma((8,)), dma((nz,)), dma((nz,)), dma((nrow,)), dma((nrow,)),
            dma((nz, PIECES // nrow, 2)), dma((nz, PIECES // nrow, 2)), dma((nz, PIECES // nrow, 2)),
            dma((2, 2, 2)), dma((3, 2, 2, 2)), dma((3, 2, 2, 2)),
            dma, dma, dma((4,)), dma((4,)), dma,
        ],
        compiler_params=pltpu.CompilerParams(
            collective_id=0, has_side_effects=True, vmem_limit_bytes=VMEM_LIMIT
        ),
    )(basis_tables, model_params, sample_values, sample_codes, gram_prev, rhs_prev)


def solution(mesh):
    placed = (
        P(None, ("row", "col")),
        P(None, ("row", "col")),
        P(None, None, "col"),
        P("col"),
        P("row", "col"),
        P("col"),
    )
    return jax.shard_map(
        functools.partial(local, mesh.shape["row"], mesh.shape["col"]),
        mesh=mesh,
        in_specs=placed,
        out_specs=(P("row", "col"), P("col")),
        check_vma=False,
    )
```

```python
import functools
import math

import jax
import jax.numpy as jnp
from jax import lax
from jax.experimental import pallas as pl
from jax.experimental.pallas import tpu as pltpu
from jax.sharding import PartitionSpec as P

MAXDEG = 64
MESH = pl.DeviceIdType.MESH
VMEM_LIMIT = 52 * 1024 * 1024
NT = (((1,), (1,)), ((), ()))
SIDE = 16
PARTS = ((0, 32), (32, 16))
PIECES = 8
UNROLL = 4


def kernel(
    nrow, ncol,
    basis_ref, params_ref, values_ref, codes_ref, prev_ref, rhs_prev_ref,
    gram_ref, rhs_ref,
    own, tab, zbuf, part, land1, tot1, land2, sums, slots, samples,
    turned, grown, hots, design, weighted, away, back,
    s1_send, s1_recv, s2_send, s2_recv,
    g1_send, g1_recv, g2_send, g2_recv, g3_send, g3_recv,
    z_send, z_recv, x_send, x_recv, y_send, y_recv,
    w_send, w_recv, p_send, p_recv, prev_sem,
):
    f32, bf16 = jnp.float32, jnp.bfloat16
    nz = ncol // 8
    row, col = lax.axis_index("row"), lax.axis_index("col")
    x, zlo = row // 2, row % 2
    zhi, yk = col // 8, col % 8
    y, core = yk // 2, yk % 2
    ncell, width = basis_ref.shape[1:]
    piece = width // PIECES
    share = PIECES // nrow
    quarter = 4 * piece
    tiles = values_ref.shape[1]
    tile = nrow * ncol
    total = tiles * tile
    mine = tiles // nrow
    scale = 1.0 / math.sqrt(total)

    def remote(src, dst, ssem, rsem, device):
        return pltpu.make_async_remote_copy(
            src_ref=src, dst_ref=dst, send_sem=ssem, recv_sem=rsem, device_id=device, device_id_type=MESH
        )

    left = (row, zhi * 8 + 2 * ((y + 3) % 4) + core)
    right = (row, zhi * 8 + 2 * ((y + 1) % 4) + core)
    sibling = (row, zhi * 8 + 2 * y + 1 - core)
    col_peers = [(row, (col + d) % ncol) for d in range(ncol)]
    row_peers = [((row + d) % nrow, col) for d in range(nrow)]
    near = [(row, zhi * 8 + (yk + d) % 8) for d in range(8)]
    far = [(row, ((zhi + d) % nz) * 8 + yk) for d in range(nz)]
    other = row + 1 - 2 * zlo
    hand = [(other, far[d][1]) if 2 * d == nz else far[d] for d in range(nz)]
    handed = [other if 2 * d == nz else row for d in range(nz)]
    parity = y % 2
    blocks = [(par, e) for par in range(2) for e in range(2)]
    offsets = (0, 3, 1, 2)

    barrier = pltpu.get_barrier_semaphore()
    greeted = col_peers[1:] + row_peers[1:] + [hand[d] for d in range(1, nz) if 2 * d == nz]
    for peer in greeted:
        pl.semaphore_signal(barrier, inc=1, device_id=peer, device_id_type=MESH)

    selves = 0
    for par, e in blocks:
        giver = (2 * y + e) // share
        if nz > 1:
            giver = jnp.where(2 * ((x - zhi + nz) % nz) == nz, giver + 1 - 2 * (giver % 2), giver)
        place = zhi * 8 + 2 * (2 * zlo + par) + core
        to_self = (giver == row) & (place == col)
        selves = selves + to_self.astype(jnp.int32)

        @pl.when(jnp.logical_not(to_self))
        def _():
            pl.semaphore_signal(barrier, inc=1, device_id=(giver, place), device_id_type=MESH)

    prev_copy = pltpu.make_async_copy(prev_ref, gram_ref, prev_sem)
    prev_copy.start()

    slots[row] = jnp.concatenate(
        [values_ref[i : i + 1, :] for i in range(4)]
        + [codes_ref[i : i + 1, :].astype(f32) for i in range(2)]
        + [jnp.zeros((1, 128 - 6 * tiles), f32)],
        axis=1,
    )
    for a in range(2):
        whole = jnp.concatenate(
            [basis_ref[a, :, 128 * j : 128 * (j + 1)].astype(f32).T for j in range(width // 128)], axis=0
        ).astype(bf16)
        for p in range(PIECES):
            for begin, rows in PARTS:
                own[p, 2 * begin + a * rows : 2 * begin + (a + 1) * rows] = whole[
                    piece * p + begin : piece * p + begin + rows
                ]

    pl.semaphore_wait(barrier, len(greeted) + len(blocks) - selves)

    s1 = [remote(slots.at[row], slots.at[row], s1_send.at[d], s1_recv.at[d], row_peers[d]) for d in range(1, nrow)]
    for copy in s1:
        copy.start()

    def half(ref, u):
        begin, rows = PARTS[u]
        return ref.at[pl.ds(2 * begin, 2 * rows)]

    def pass_z(d, u):
        return [
            remote(half(own.at[row * share + m], u), half(zbuf.at[nz - d, m], u), z_send.at[d, m, u], z_recv.at[nz - d, m, u], hand[d])
            for m in range(share)
        ]

    def pass_x(d, u):
        to = 2 * ((zhi + d) % nz) + y // 2
        for m in range(share):
            p = handed[d] * share + m
            target = zhi * 8 + 2 * (p // 2) + core
            source = half(own.at[p] if d == 0 else zbuf.at[d, m], u)
            place = half(tab.at[0, parity, p % 2], u)
            arrived = x_recv.at[parity, p % 2, u]
            to_self = (to == row) & (target == col)

            @pl.when(jnp.logical_not(to_self))
            def _():
                remote(source, place, x_send.at[d, m, u], arrived, (to, target)).start()

            @pl.when(to_self)
            def _():
                pltpu.make_async_copy(source, place, arrived).start()

    zs = [[copy for d in range(1, nz) for copy in pass_z(d, u)] for u in range(2)]
    for copy in zs[0]:
        copy.start()
    for u in range(2):
        pass_x(0, u)

    rest = params_ref[...].reshape(1, width)
    terms = []
    for n in range(3):
        terms.append(rest.astype(bf16).astype(f32))
        rest = rest - terms[-1]
    terms = jnp.concatenate(terms + [jnp.zeros((SIDE - 3, width), f32)], axis=0).astype(bf16)

    for copy in s1:
        copy.wait_recv()
    for i in range(nrow):
        samples[col, pl.ds(i, 1)] = slots[i]
    s2 = [
        remote(samples.at[col], samples.at[col], s2_send.at[d], s2_recv.at[d], col_peers[d]) for d in range(1, ncol)
    ]
    for copy in s2:
        copy.start()
    for copy in zs[1]:
        copy.start()

    def pass_zx(u):
        for d in sorted(range(1, nz), key=lambda d: 2 * d == nz):
            for m in range(share):
                here = half(zbuf.at[d, m], u)
                remote(here, here, z_send.at[d, m, u], z_recv.at[d, m, u], hand[d]).wait_recv()
            pass_x(d, u)

    def pass_y(u):
        for par, e in blocks:
            here = half(tab.at[0, par, e], u)
            pltpu.make_async_copy(here, here, x_recv.at[par, e, u]).wait()
            remote(here, half(tab.at[1, par, e], u), y_send.at[0, par, e, u], y_recv.at[0, par, e, u], right).start()
            remote(here, half(tab.at[2, par, e], u), y_send.at[1, par, e, u], y_recv.at[1, par, e, u], left).start()

    def arrive(g, par, e, u):
        here = half(tab.at[g, par, e], u)
        remote(here, here, y_send.at[0, par, e, u], y_recv.at[g - 1, par, e, u], right).wait_recv()

    def pass_on(u):
        for par in range(2):
            for g, to in ((1, right), (2, left)):
                e = g - 1
                arrive(g, par, e, u)
                remote(
                    half(tab.at[g, par, e], u), half(tab.at[3, par, e], u), y_send.at[2, par, e, u], y_recv.at[2, par, e, u], to
                ).start()

    def field(number, k):
        return turned[pl.ds(number * tiles + k, 1), :]

    def span(k):
        return pl.ds(pl.multiple_of(k * tile, tile), tile)

    exponent = (lax.broadcasted_iota(jnp.int32, (MAXDEG, tile), 0) + 1).astype(f32)
    cells = lax.broadcasted_iota(jnp.int32, (ncell, tile), 0).astype(jnp.int16)
    reach = grown.shape[2]

    def build_own(number, carry):
        k = (number + row * mine) % tiles
        hot = jnp.where(cells == field(4, k).astype(jnp.int32).astype(jnp.int16), jnp.bfloat16(1), jnp.bfloat16(0))
        hots[k] = hot
        grow = jnp.exp(field(2, k) * exponent)
        grows = []
        for a in range(2):
            value = grow * field(a, k)
            value = jnp.concatenate([value, value], axis=0)
            grown[a, k] = value[:reach]
            grows.append(value)
        picked = jnp.dot(own[...].reshape(2 * width, ncell), hot, preferred_element_type=f32)
        for p in range(PIECES):
            for begin, rows in PARTS:
                first = 2 * (piece * p + begin)
                at = (p * piece + begin) % MAXDEG
                weighted[0, p * piece + begin : p * piece + begin + rows, span(k)] = (
                    picked[first : first + rows] * grows[0][at : at + rows]
                    + picked[first + rows : first + 2 * rows] * grows[1][at : at + rows]
                ).astype(bf16)
        return carry

    def mixed(picked, k, begin, rows):
        at = pl.ds(pl.multiple_of(begin % MAXDEG, 16), rows)
        return (picked[:rows] * grown[0, k, at] + picked[rows:] * grown[1, k, at]).astype(bf16)

    def weigh(k, carry):
        weighted[0, :, span(k)] = (weighted[0, :, span(k)].astype(f32) * field(5, k)).astype(bf16)
        rest = field(3, k)
        split = []
        for n in range(3):
            split.append(rest.astype(bf16).astype(f32))
            rest = rest - split[-1]
        split.append(jnp.zeros((SIDE - 3, tile), f32))
        design[3 * quarter : 3 * quarter + SIDE, span(k)] = jnp.concatenate(split, axis=0).astype(bf16)
        return carry

    def origin(g, e):
        return 2 * ((y + offsets[g]) % 4) + e

    def first_row(g):
        return g * quarter + (SIDE if g > 2 else 0)

    def build_rows(groups, parts):
        lo = PARTS[parts[0]][0]
        hi = sum(PARTS[parts[-1]])
        size = 2 * (hi - lo)

        def body(k, carry):
            lhs = tab[groups[0] : groups[-1] + 1, :, :, 2 * lo : 2 * hi].reshape(4 * size * len(groups), ncell)
            picked = jnp.dot(lhs, hots[k], preferred_element_type=f32)
            for j, g in enumerate(groups):
                for n, (par, e) in enumerate(blocks):
                    for u in parts:
                        begin, rows = PARTS[u]
                        at = first_row(g) + n * piece + begin
                        first = size * (4 * j + n) + 2 * (begin - lo)
                        design[at : at + rows, span(k)] = mixed(
                            picked[first : first + 2 * rows], k, origin(g, e) * piece + begin, rows
                        )
            return carry

        lax.fori_loop(0, tiles, body, 0, unroll=UNROLL)

    def collect(groups, which, product):
        for j, g in enumerate(groups):
            for n, (par, e) in enumerate(blocks):
                at = pl.ds(pl.multiple_of((2 * par + which) * width + origin(g, e) * piece, 16), piece)
                begin = j * quarter + n * piece
                gram_ref[at, :] = gram_ref[at, :] + scale * product[begin : begin + piece]

    def swap(groups):
        at, g = pl.ds(groups[0] * quarter, len(groups) * quarter), groups[0]
        return remote(away.at[at], back.at[at], p_send.at[g], p_recv.at[g], sibling)

    def form(groups):
        count = len(groups) * quarter
        rows = count + (SIDE if groups[0] == 0 else 0)
        first = first_row(groups[0])
        if groups[-1] == 3:
            lhs = design[first : first + rows]
            away[groups[0] * quarter : groups[0] * quarter + count] = lax.dot_general(
                lhs, weighted[1], NT, preferred_element_type=f32
            )
            swap(groups).start()
            collect(groups, core, lax.dot_general(lhs, weighted[0], NT, preferred_element_type=f32))
            return
        both = weighted[...].reshape(2 * width, total)
        product = lax.dot_general(design[first : first + rows], both, NT, preferred_element_type=f32)
        away[groups[0] * quarter : groups[0] * quarter + count] = product[:count, width:]
        swap(groups).start()
        collect(groups, core, product[:count, :width])
        if groups[0] == 0:
            rhs_ref[...] = rhs_prev_ref[...] + scale * jnp.sum(product[count : count + 8, :width], axis=0)

    def finish(groups):
        swap(groups).wait_recv()
        collect(groups, 1 - core, back[groups[0] * quarter : (groups[-1] + 1) * quarter])

    def some(body, number, parts):
        lax.fori_loop(number * tiles // parts, (number + 1) * tiles // parts, body, 0, unroll=UNROLL)

    pass_zx(0)
    for copy in s2:
        copy.wait_recv()
    turned[...] = samples[...].reshape(tile, 128).T
    some(build_own, 0, 4)
    early = -(-4 * mine // tiles)
    for n in range(1, early):
        some(build_own, n, 4)
    for j in range(mine):
        value = jnp.dot(terms, weighted[0, :, span(row * mine + j)], preferred_element_type=f32)
        part[j : j + 1, :] = jnp.sum(value[:8], axis=0, keepdims=True)
    g1 = [remote(part, land1.at[d], g1_send.at[d], g1_recv.at[d], near[d]) for d in range(1, 8)]
    for copy in g1:
        copy.start()
    for n in range(early, 2):
        some(build_own, n, 4)
    pass_zx(1)
    some(build_own, 2, 4)
    for copy in g1:
        copy.wait_recv()
    amount = part[...]
    for d in range(1, 8):
        amount = amount + land1[d]
    tot1[...] = amount
    g2 = [remote(tot1, land2.at[d], g2_send.at[d], g2_recv.at[d], far[d]) for d in range(1, nz)]
    for copy in g2:
        copy.start()
    some(build_own, 3, 4)
    pass_y(0)
    build_rows((0,), (0,))
    for copy in g2:
        copy.wait_recv()
    amount = tot1[...]
    for d in range(1, nz):
        amount = amount + land2[d]
    sums[row] = amount
    g3 = [remote(sums.at[row], sums.at[row], g3_send.at[d], g3_recv.at[d], row_peers[d]) for d in range(1, nrow)]
    for copy in g3:
        copy.start()
    pass_y(1)
    build_rows((0,), (1,))
    pass_on(0)
    for copy in g3:
        copy.wait_recv()

    residual = turned[3 * tiles : 4 * tiles, :] - jnp.concatenate([sums[r] for r in range(nrow)], axis=0)
    group = turned[5 * tiles : 6 * tiles, :]
    size = jnp.abs(residual)
    limit = jnp.zeros_like(size)
    for number in range(2):
        hot = (group == float(number)).astype(f32)
        count = jnp.sum(jnp.sum(hot, axis=0, keepdims=True), axis=1, keepdims=True)
        spread = jnp.sum(jnp.sum(hot * size, axis=0, keepdims=True), axis=1, keepdims=True)
        limit = limit + hot * (1.345 * spread / jnp.maximum(count, 1.0))
    turned[3 * tiles : 4 * tiles, :] = residual
    turned[5 * tiles : 6 * tiles, :] = limit / jnp.maximum(size, limit)
    some(weigh, 0, 1)
    w_copy = remote(weighted.at[0], weighted.at[1], w_send, w_recv, sibling)
    w_copy.start()

    for par in range(2):
        arrive(1, par, 1, 0)
        arrive(2, par, 0, 0)
    build_rows((1, 2), (0,))
    pass_on(1)
    for par in range(2):
        arrive(1, par, 1, 1)
        arrive(2, par, 0, 1)
    build_rows((1, 2), (1,))
    w_copy.wait_recv()
    prev_copy.wait()
    form((0, 1, 2))
    for par, e in blocks:
        for u in range(2):
            arrive(3, par, e, u)
    build_rows((3,), (0, 1))
    form((3,))
    finish((0, 1, 2))
    finish((3,))

    for copy in s1 + s2 + g1 + g2 + g3 + zs[0] + zs[1] + [w_copy]:
        copy.wait_send()
    for u in range(2):
        for d in range(nz):
            to = 2 * ((zhi + d) % nz) + y // 2
            for m in range(share):
                p = handed[d] * share + m
                target = zhi * 8 + 2 * (p // 2) + core

                @pl.when((to != row) | (target != col))
                def _():
                    here = half(own.at[p], u)
                    remote(here, here, x_send.at[d, m, u], x_recv.at[0, 0, u], (to, target)).wait_send()

        for par, e in blocks:
            for n in range(3):
                here = half(tab.at[n, par, e], u)
                remote(here, here, y_send.at[n, par, e, u], y_recv.at[0, par, e, u], right).wait_send()
    for groups in ((0, 1, 2), (3,)):
        swap(groups).wait_send()


def local(nrow, ncol, sample_values, sample_codes, basis_tables, model_params, gram_prev, rhs_prev):
    ncell, width = basis_tables.shape[1:]
    nz = ncol // 8
    tiles = sample_values.shape[1]
    tile = nrow * ncol
    total = tile * tiles
    piece = width // PIECES
    dma = pltpu.SemaphoreType.DMA
    vmem = pl.BlockSpec(memory_space=pltpu.VMEM)
    anywhere = pl.BlockSpec(memory_space=pl.ANY)
    f32, bf16 = jnp.float32, jnp.bfloat16
    return pl.pallas_call(
        functools.partial(kernel, nrow, ncol),
        out_shape=(
            pltpu.VMEM(gram_prev.shape, f32),
            pltpu.VMEM(rhs_prev.shape, f32),
        ),
        in_specs=[vmem, vmem, vmem, vmem, anywhere, vmem],
        out_specs=(vmem, vmem),
        scratch_shapes=[
            pltpu.VMEM((PIECES, 2 * piece, ncell), bf16),
            pltpu.VMEM((4, 2, 2, 2 * piece, ncell), bf16),
            pltpu.VMEM((nz, PIECES // nrow, 2 * piece, ncell), bf16),
            pltpu.VMEM((tiles // nrow, tile), f32),
            pltpu.VMEM((8, tiles // nrow, tile), f32),
            pltpu.VMEM((tiles // nrow, tile), f32),
            pltpu.VMEM((nz, tiles // nrow, tile), f32),
            pltpu.VMEM((nrow, tiles // nrow, tile), f32),
            pltpu.VMEM((nrow, 1, 128), f32),
            pltpu.VMEM((ncol, nrow, 128), f32),
            pltpu.VMEM((128, tile), f32),
            pltpu.VMEM((2, tiles, MAXDEG + piece, tile), f32),
            pltpu.VMEM((tiles, ncell, tile), bf16),
            pltpu.VMEM((2 * width + SIDE, total), bf16),
            pltpu.VMEM((2, width, total), bf16),
            pltpu.VMEM((2 * width, width), f32),
            pltpu.VMEM((2 * width, width), f32),
            dma((nrow,)), dma((nrow,)), dma((ncol,)), dma((ncol,)),
            dma((8,)), dma((8,)), dma((nz,)), dma((nz,)), dma((nrow,)), dma((nrow,)),
            dma((nz, PIECES // nrow, 2)), dma((nz, PIECES // nrow, 2)), dma((nz, PIECES // nrow, 2)),
            dma((2, 2, 2)), dma((3, 2, 2, 2)), dma((3, 2, 2, 2)),
            dma, dma, dma((4,)), dma((4,)), dma,
        ],
        compiler_params=pltpu.CompilerParams(
            collective_id=0, has_side_effects=True, vmem_limit_bytes=VMEM_LIMIT
        ),
    )(basis_tables, model_params, sample_values, sample_codes, gram_prev, rhs_prev)


def solution(mesh):
    placed = (
        P(None, ("row", "col")),
        P(None, ("row", "col")),
        P(None, None, "col"),
        P("col"),
        P("row", "col"),
        P("col"),
    )
    return jax.shard_map(
        functools.partial(local, mesh.shape["row"], mesh.shape["col"]),
        mesh=mesh,
        in_specs=placed,
        out_specs=(P("row", "col"), P("col")),
        check_vma=False,
    )
```
